128 devices in a mesh: grp: 8 (over y_lo, z), col: 16 (over y_hi, x, core).
Axes of the slice: x: 4, y: 4 (y_hi: 2, y_lo: 2; y = y_hi * 2 + y_lo), z: 4, core: 2. Of those that a mesh axis runs over, the one named last changes fastest.
Arguments:
- tokens: bfloat16 [1024, 6144], P('grp', 'col'), may hold values from -6 to 6
- grad_out: bfloat16 [1024, 6144], P('grp', 'col'), may hold values from -6 to 6
- expert_ids: int32 [1024, 2], P('grp'), may hold values from 0 to 3, all different within a row; in each aligned block of 128 rows (0 to 127, 128 to 255, ...) at most 80 rows name the same one
- gate_num: int32 [1024], P('grp'), may hold values from 1 to 63
- gate_weight: bfloat16 [6144, 32768], P(None, ('grp', 'col')), may hold values from -0.078125 to 0.078125
- up_weight: bfloat16 [6144, 32768], P(None, ('grp', 'col')), may hold values from -0.078125 to 0.078125
- down_weight: bfloat16 [32768, 6144], P(('grp', 'col')), may hold values from -0.0625 to 0.0625
Outputs:
- layer_out: bfloat16 [1024, 6144], P('grp', 'col')
- grad_tokens: bfloat16 [1024, 6144], P('grp', 'col')
- grad_gate: bfloat16 [6144, 32768], P(None, ('grp', 'col'))
- grad_up: bfloat16 [6144, 32768], P(None, ('grp', 'col'))
- grad_down: bfloat16 [32768, 6144], P(('grp', 'col'))
The draws below stay inside these ranges and needn't reach their ends.
Inputs may be any that keep to these rules, and one draw needn't show every extreme that they name: `expert_ids`: the two ids of a token differ. In each aligned block of 128 tokens (those of one grp index) no expert is named by more than 80 tokens, a bound that some block reaches.
All inputs are finite; a program needn't handle non-finite values.
Results may differ from the reference program's by a relative error of at most 0.02.
Values may be sent and summed in bfloat16 or wider, within the bound.
A program may use at most 192 MiB of HBM per device.

```python
import math
import jax
import jax.numpy as jnp
import numpy as np
from jax import lax

D = 6144
FF = 8192
SPAN = 2
TOK_GRP = 128
EXPERTS = 4
CAP = 80
TOKENS = 1024
N_GRP = 8
N_COL = 16


def with_ends(result, key, low, high):
    longest = result.shape.index(max(result.shape))
    spots = []
    for shift in (0, 1):
        where = [jax.random.randint(jax.random.fold_in(key, axis), (), 0, length) for axis, length in enumerate(result.shape)]
        where[longest] = (where[longest] + shift) % result.shape[longest]
        spots.append(tuple(where))
    return result.at[spots[0]].set(low).at[spots[1]].set(high)


def levels(own_key, shape, cuts, smallest, high):
    level, own = 1.0, jax.random.fold_in(own_key, 6)
    for axis_at, shards_of in cuts:
        steps = jnp.exp(jax.random.uniform(jax.random.fold_in(own, axis_at), (shards_of,), jnp.float32, smallest / len(cuts), high / len(cuts)))
        level = level * jnp.repeat(steps, shape[axis_at] // shards_of).reshape([-1 if axis == axis_at else 1 for axis in range(len(shape))])
    return level


def assign_block(own_key, own, number, rows, number_of, top, bound, skew):
    sequence = jax.random.permutation(own_key, number_of)
    heavy_load, usual = shares(number_of, rows * top, bound, skew, True), shares(number_of, rows * top, bound, skew, False)
    places = jnp.arange(number_of)

    def named(lengths, turn):
        used = int((lengths > 0).sum())
        fixed = max(1, used // 4)
        passed = fixed + (places - fixed + turn * (used - fixed)) % max(1, number_of - fixed)
        return jnp.zeros((number_of,), jnp.int32).at[sequence[jnp.where(places < fixed, places, passed)]].set(jnp.asarray(lengths, jnp.int32))

    lengths = jnp.where(number % 4 == 0, named(heavy_load, number // 4), named(usual, number - number // 4 - 1))
    mixed = jax.random.permutation(jax.random.fold_in(own, 3), number_of)
    giver, sink = mixed[0:number_of // 2 * 2:2], mixed[1:number_of // 2 * 2:2]
    room = jnp.minimum(lengths[giver] - 1, bound - lengths[sink]) // 2
    room = jnp.where((giver == sequence[0]) | (sink == sequence[0]) | (lengths[sink] == 0), 0, jnp.maximum(room, 0))
    passed = jax.random.randint(jax.random.fold_in(own, 4), (number_of // 2,), 0, 1 << 20) % (room + 1)
    lengths = lengths.at[giver].add(-passed).at[sink].add(passed)
    members = jnp.searchsorted(jnp.cumsum(lengths), jnp.arange(rows * top), side="right").astype(jnp.int32)
    listing = members.reshape(top, rows).T
    listing = listing[jax.random.permutation(jax.random.fold_in(own, 1), rows)]
    turn = jax.random.randint(jax.random.fold_in(own, 2), (rows, 1), 0, top)
    return jnp.take_along_axis(listing, (jnp.arange(top)[None, :] + turn) % top, axis=1)


def shares(amount, total, bound, slope, full):
    portions = [(1 << 20) // math.isqrt(rank ** slope) + 1 for rank in range(1, amount + 1)]
    largest = bound if full else min(bound, max(-(-total // amount), total * portions[0] // sum(portions)))
    least = 1 if total - largest >= amount - 1 else 0
    counts, rest = [largest] + [least] * (amount - 1), total - largest - least * (amount - 1)
    while rest > 0:
        free = [i for i in range(1, amount) if counts[i] < largest] or [i for i in range(1, amount) if counts[i] < bound]
        pool, left = sum([portions[i] for i in free]), rest
        for i in free:
            more = min(bound - counts[i], max(1, left * portions[i] // pool), rest)
            counts[i] = counts[i] + more
            rest = rest - more
    return np.array(counts)


def noise(rng, extent, scale, limit, cuts=(), held_as=jnp.bfloat16):
    loudness = levels(rng, extent, cuts, -0.22, 0.18) if cuts else 1.0
    values = jax.random.normal(rng, extent, jnp.float32) * scale * loudness
    return jnp.minimum(jnp.maximum(values, -limit), limit).astype(held_as)


def setup_inputs(seed: int = 0) -> dict:
    arg_keys = jax.random.split(jax.random.key(seed), 8)
    tokens = noise(arg_keys[0], (TOKENS, D), 1.0, 6.0, ((0, 8), (1, 16)))
    grad_out = noise(arg_keys[1], (TOKENS, D), 1.0, 6.0, ((0, 8), (1, 16)))
    expert_ids_keys = jax.random.split(jax.random.fold_in(arg_keys[2], 1), TOKENS // TOK_GRP)
    expert_ids_turns = jax.random.permutation(jax.random.fold_in(arg_keys[2], 3), TOKENS // TOK_GRP)
    expert_ids = jax.vmap(lambda own, number: assign_block(jax.random.fold_in(arg_keys[2], 2), own, number, TOK_GRP, EXPERTS, 2, CAP, 2))(expert_ids_keys, expert_ids_turns).reshape((TOKENS, 2))
    gate_num = with_ends(jax.random.randint(arg_keys[3], (TOKENS,), 1, 64), jax.random.fold_in(arg_keys[3], 1), 1, 63).astype(jnp.int32)
    gate_weight = noise(arg_keys[4], (D, EXPERTS * FF), D ** -0.5, 0.078125, ((1, 128),))
    up_weight = noise(arg_keys[5], (D, EXPERTS * FF), D ** -0.5, 0.078125, ((1, 128),))
    down_weight = noise(arg_keys[6], (EXPERTS * FF, D), FF ** -0.5, 0.0625, ((0, 128),))
    return dict(tokens=tokens, grad_out=grad_out, expert_ids=expert_ids, gate_num=gate_num, gate_weight=gate_weight, up_weight=up_weight, down_weight=down_weight)


def routing_tables(expert_ids, gate_num, experts, capacity):
    count = expert_ids.shape[0]
    flat_ids = expert_ids.reshape(-1).astype(jnp.int32)
    labels = jnp.arange(experts, dtype=jnp.int32)
    onehot = (flat_ids[:, None] == labels[None, :]).astype(jnp.int32)
    earlier = (jnp.cumsum(onehot, axis=0) - onehot).astype(jnp.int32)
    position = jnp.sum(earlier * onehot, axis=1).astype(jnp.int32)
    target = (flat_ids * capacity + position).astype(jnp.int32)
    share = gate_num.astype(jnp.float32) / 64.0
    pair_weight = jnp.stack([share, 1.0 - share], axis=1).reshape(-1)
    slots = jnp.arange(experts * capacity, dtype=jnp.int32)
    matches = slots[:, None] == target[None, :]
    chosen = jnp.any(matches.reshape(experts * capacity, count, 2), axis=2)
    weighted = jnp.where(matches, pair_weight[None, :], jnp.zeros_like(pair_weight)[None, :])
    slot_weight = jnp.sum(weighted, axis=1)
    return target, pair_weight, chosen, slot_weight


def combine(buffer, target, pair_weight, count):
    picked = jnp.take(buffer, target, axis=0)
    return jnp.sum(picked.reshape(count, 2, -1) * pair_weight.reshape(count, 2, 1), axis=1)


def rounded(value):
    return lax.optimization_barrier(value.astype(jnp.bfloat16)).astype(jnp.float32)


def reference(tokens, grad_out, expert_ids, gate_num, gate_weight, up_weight, down_weight):
    pieces = SPAN * N_COL
    block = FF // pieces
    rows = N_GRP * CAP
    target, pair_weight, chosen, slot_weight = jax.vmap(
        lambda ids, nums: routing_tables(ids, nums, EXPERTS, CAP))(
        expert_ids.reshape(N_GRP, TOK_GRP, 2), gate_num.reshape(N_GRP, TOK_GRP))
    picker = chosen.astype(jnp.float32)
    moved = jnp.einsum("gst,gtd->gsd", picker, tokens.reshape(N_GRP, TOK_GRP, D).astype(jnp.float32)).astype(jnp.bfloat16)
    scaled = jnp.einsum("gst,gtd->gsd", picker, grad_out.reshape(N_GRP, TOK_GRP, D).astype(jnp.float32))
    scaled = (scaled * slot_weight[:, :, None]).astype(jnp.bfloat16)
    all_rows = moved.reshape(N_GRP, EXPERTS, CAP, D).transpose(1, 0, 2, 3).reshape(EXPERTS, rows, D)
    all_grads = scaled.reshape(N_GRP, EXPERTS, CAP, D).transpose(1, 0, 2, 3).reshape(EXPERTS, rows, D)
    outputs, backs, gate_grads, up_grads, down_grads = [], [], [], [], []
    for expert in range(EXPERTS):
        token_rows = all_rows[expert]
        grad_rows = all_grads[expert]
        gate_cols = gate_weight[:, expert * FF:(expert + 1) * FF]
        up_cols = up_weight[:, expert * FF:(expert + 1) * FF]
        down_part = down_weight[expert * FF:(expert + 1) * FF, :]
        gate_act = jnp.dot(token_rows, gate_cols, preferred_element_type=jnp.float32)
        up_act = jnp.dot(token_rows, up_cols, preferred_element_type=jnp.float32)
        sigmoid_gate = jax.nn.sigmoid(gate_act)
        hidden = (gate_act * sigmoid_gate * up_act).astype(jnp.bfloat16)
        hidden_blocks = hidden.reshape(rows, pieces, block).transpose(1, 0, 2)
        down_blocks = down_part.reshape(pieces, block, D)

        def add_out(total, pair):
            return total + rounded(jnp.dot(pair[0], pair[1], preferred_element_type=jnp.float32)), None

        expert_out, _ = lax.scan(add_out, jnp.zeros((rows, D), jnp.float32), (hidden_blocks, down_blocks))
        grad_hidden = jnp.dot(grad_rows, down_part.T, preferred_element_type=jnp.float32)
        grad_gate_act = (grad_hidden * up_act * sigmoid_gate * (1.0 + gate_act * (1.0 - sigmoid_gate))).astype(jnp.bfloat16)
        grad_up_act = (grad_hidden * gate_act * sigmoid_gate).astype(jnp.bfloat16)
        down_grads.append(jnp.dot(hidden.T, grad_rows, preferred_element_type=jnp.float32).astype(jnp.bfloat16))
        gate_grads.append(jnp.dot(token_rows.T, grad_gate_act, preferred_element_type=jnp.float32).astype(jnp.bfloat16))
        up_grads.append(jnp.dot(token_rows.T, grad_up_act, preferred_element_type=jnp.float32).astype(jnp.bfloat16))
        gate_blocks = gate_cols.reshape(D, pieces, block).transpose(1, 0, 2)
        up_blocks = up_cols.reshape(D, pieces, block).transpose(1, 0, 2)
        ggate_blocks = grad_gate_act.reshape(rows, pieces, block).transpose(1, 0, 2)
        gup_blocks = grad_up_act.reshape(rows, pieces, block).transpose(1, 0, 2)

        def add_back(total, quad):
            term = jnp.dot(quad[0], quad[1].T, preferred_element_type=jnp.float32)
            term = term + jnp.dot(quad[2], quad[3].T, preferred_element_type=jnp.float32)
            return total + rounded(term), None

        expert_back, _ = lax.scan(add_back, jnp.zeros((rows, D), jnp.float32),
                                  (ggate_blocks, gate_blocks, gup_blocks, up_blocks))
        outputs.append(expert_out)
        backs.append(expert_back)
    out_buffer = jnp.stack(outputs).reshape(EXPERTS, N_GRP, CAP, D).transpose(1, 0, 2, 3).reshape(N_GRP, EXPERTS * CAP, D)
    back_buffer = jnp.stack(backs).reshape(EXPERTS, N_GRP, CAP, D).transpose(1, 0, 2, 3).reshape(N_GRP, EXPERTS * CAP, D)
    layer_out = jax.vmap(lambda buf, tgt, wts: combine(buf, tgt, wts, TOK_GRP))(out_buffer, target, pair_weight)
    grad_tokens = jax.vmap(lambda buf, tgt, wts: combine(buf, tgt, jnp.ones_like(wts), TOK_GRP))(back_buffer, target, pair_weight)
    return (layer_out.reshape(TOKENS, D).astype(jnp.bfloat16),
            grad_tokens.reshape(TOKENS, D).astype(jnp.bfloat16),
            jnp.concatenate(gate_grads, axis=1),
            jnp.concatenate(up_grads, axis=1),
            jnp.concatenate(down_grads, axis=0))
```

```python
import functools

import jax
import jax.numpy as jnp
from jax import lax
from jax.experimental import pallas as pl
from jax.experimental.pallas import tpu as pltpu
from jax.sharding import PartitionSpec as P

MESH = pl.DeviceIdType.MESH
BF = jnp.bfloat16
F32 = jnp.float32
CHUNKS = 4
ROWS_TOP = (((0,), (0,)), ((), ()))
ROWS_BOTH = (((1,), (1,)), ((), ()))


def kernel(cap, f, h, names,
           meta, tok, gout, wg, wu, wd,
           lo, gt, gg, gu, gd,
           picks, sent, tbuf, gbuf, wgu, wdn, act_mine, act_theirs, hid, gact, pout, pback,
           ax1, ax2, az, ay, by, bx1, bx2, bz, home, gwt, gdt, ss, rs, ls):
    d2 = 8 * f
    grp, col = lax.axis_index("grp"), lax.axis_index("col")
    yl, z = grp // 4, grp % 4
    zh, zl = z // 2, z % 2
    yh, x, c = col // 8, (col // 2) % 4, col % 2
    xr, xl, xo = (x + 1) % 4, (x + 3) % 4, (x + 2) % 4

    def dev(yl=yl, z=z, yh=yh, x=x, c=c):
        return (yl * 4 + z, (yh * 4 + x) * 2 + c)

    right, left = dev(x=xr), dev(x=xl)
    other_y, other_z, other_c = dev(yh=1 - yh), dev(z=z + 1 - 2 * zl), dev(c=1 - c)

    def source(k):
        dy, dz = k // 2, k % 2
        return dict(yl=1 - yl if dy else yl, z=3 - z if dz else z)

    counter = [0]
    started = []

    def send(src, dst, target):
        i = counter[0]
        counter[0] += 1
        copy = pltpu.make_async_remote_copy(
            src_ref=src, dst_ref=dst, send_sem=ss.at[i], recv_sem=rs.at[i],
            device_id=target, device_id_type=MESH)
        copy.start()
        started.append(copy)
        return copy

    def got(copies):
        for copy in copies:
            copy.wait_recv()

    def lanes(off, n):
        return pl.ds(pl.multiple_of(off, 128), n)

    def rws(off, n):
        return pl.ds(pl.multiple_of(off, 16), n)

    def off_a(x, yh):
        return (x * 2 + yh) * f

    def off_b(yh, x):
        return (yh * 4 + x) * f

    def add_into(dst, row, n, off, width, *srcs):
        @pl.loop(0, n // 16)
        def _(i):
            at = (rws(row + i * 16, 16), lanes(off, width))
            total = dst[at].astype(F32)
            for src in srcs:
                total = total + src[rws(i * 16, 16), :].astype(F32)
            dst[at] = total.astype(BF)

    barrier = pltpu.get_barrier_semaphore()
    partners = [right, left, other_y, other_z, other_c] + [dev(**source(k)) for k in (1, 2, 3)]
    for partner in partners:
        pl.semaphore_signal(barrier, inc=1, device_id=partner, device_id_type=MESH)
    pl.semaphore_wait(barrier, len(partners))

    for y in range(2):
        for q, w in enumerate((wg, wu)):
            at = (slice(None), y, slice(None), lanes(2 * h * q + h * c, h))
            pltpu.make_async_copy(w.at[y, :, c], wgu.at[at], ls.at[0]).start()
            pltpu.make_async_remote_copy(
                src_ref=w.at[y, :, 1 - c], dst_ref=wgu.at[at], send_sem=ls.at[1], recv_sem=ls.at[2],
                device_id=other_c, device_id_type=MESH).start()
    for p in range(8):
        at = (rws(h * c, h), pl.ds(p * f, f))
        pltpu.make_async_copy(wd.at[:, lanes((p * 2 + c) * f, f)], wdn.at[at], ls.at[3]).start()
        pltpu.make_async_remote_copy(
            src_ref=wd.at[:, lanes((p * 2 + 1 - c) * f, f)], dst_ref=wdn.at[at], send_sem=ls.at[4], recv_sem=ls.at[5],
            device_id=other_c, device_id_type=MESH).start()

    def weights_ready():
        half_gu = wgu.at[:, :, :, pl.ds(0, 2 * h)]
        half_d = wdn.at[pl.ds(0, h)]
        for i, part in ((0, half_gu), (1, half_gu), (2, half_gu), (3, half_d), (4, half_d), (5, half_d)):
            pltpu.make_async_copy(part, part, ls.at[i]).wait()

    first, second = meta[0:1, :], meta[1:2, :]
    share = meta[2:3, :].astype(F32) / 64.0
    count = first.shape[1]
    has, weight = [], []
    for k in range(CHUNKS):
        where = source(k)
        expert = where["yl"] * 2 + where["z"] // 2
        one, two = first == expert, second == expert
        has.append(jnp.logical_or(one, two).astype(F32))
        weight.append(jnp.where(one, share, 1.0 - share))
    marks = jnp.concatenate(has + [jnp.zeros((4, count), F32)], axis=0)
    before = (lax.broadcasted_iota(jnp.int32, (count, count), 0)
              < lax.broadcasted_iota(jnp.int32, (count, count), 1)).astype(F32)
    position = jnp.dot(marks.astype(BF), before.astype(BF), preferred_element_type=F32)
    slot = lax.broadcasted_iota(jnp.int32, (cap, count), 0).astype(F32)
    for k in range(CHUNKS):
        chosen = jnp.where(slot == position[k:k + 1, :], has[k], 0.0)
        picks[0, k] = chosen.astype(BF)
        picks[1, k] = (chosen * weight[k]).astype(BF)
        sent[0, k] = jnp.dot(picks[0, k], tok[...], preferred_element_type=F32).astype(BF)
        sent[1, k] = jnp.dot(picks[1, k], gout[...], preferred_element_type=F32).astype(BF)

    pend = {}
    two = 2 * cap

    def dispatch(k):
        here = (lanes(off_a(x, yh), f), lanes(off_b(yh, x), f))
        if k == 0:
            copies = [pltpu.make_async_copy(sent.at[a, 0], buf.at[rws(zl * cap, cap), here[a]], ls.at[6 + a])
                      for a, buf in enumerate((tbuf, gbuf))]
            for copy in copies:
                copy.start()
            pend["d", k] = copies
            return
        theirs = 1 - zl if k % 2 else zl
        pend["d", k] = [send(sent.at[a, k], buf.at[rws(k * two + theirs * cap, cap), here[a]], dev(**source(k)))
                        for a, buf in enumerate((tbuf, gbuf))]

    def dispatched(k):
        if k == 0:
            for copy in pend["d", 0]:
                copy.wait()
        else:
            got(pend["d", k])

    def put(buf, row, n, off, width, target):
        at = (rws(row, n), lanes(off, width))
        return send(buf.at[at], buf.at[at], target)

    def gather_a(k, phase):
        mine, all_rows = k * two + zl * cap, k * two
        if phase == 1:
            pend["a", k] = [put(tbuf, mine, cap, off_a(x, yh), f, other_y)]
        elif phase == 2:
            got(pend["a", k])
            pend["a", k] = [put(tbuf, mine, cap, off_a(x, 0), 2 * f, other_z)]
        elif phase == 3:
            got(pend["a", k])
            pend["a", k] = [put(tbuf, all_rows, two, off_a(x, 0), 2 * f, right),
                            put(tbuf, all_rows, two, off_a(x, 0), 2 * f, left)]
        elif phase == 4:
            got(pend["a", k])
            pend["a", k] = [put(tbuf, all_rows, cap, off_a(xl, 0), 2 * f, right),
                            put(tbuf, all_rows + cap, cap, off_a(xr, 0), 2 * f, left)]
        else:
            got(pend["a", k])

    def gather_b(k, phase):
        mine, all_rows = k * two + zl * cap, k * two
        if phase == 1:
            pend["b", k] = [put(gbuf, mine, cap, off_b(yh, x), f, other_z)]
        elif phase == 2:
            got(pend["b", k])
            pend["b", k] = [put(gbuf, all_rows, two, off_b(yh, x), f, right),
                            put(gbuf, all_rows, two, off_b(yh, x), f, left)]
        elif phase == 3:
            got(pend["b", k])
            pend["b", k] = [put(gbuf, all_rows, cap, off_b(yh, xl), f, right),
                            put(gbuf, all_rows + cap, cap, off_b(yh, xr), f, left)]
        elif phase == 4:
            got(pend["b", k])
            pend["b", k] = [put(gbuf, all_rows, two, off_b(yh, 0), 4 * f, other_y)]
        else:
            got(pend["b", k])

    def project(k):
        rows = pl.ds(k * two, two)

        @pl.loop(0, 4)
        def _(n):
            w = wgu[:, :, :, lanes(n * h, h)].reshape(d2, h)
            act_mine[rows, lanes(n * h, h)] = jnp.dot(tbuf[rows, :], w, preferred_element_type=F32)

        @pl.loop(0, 2)
        def _(n):
            act_mine[rows, lanes((4 + n) * h, h)] = lax.dot_general(
                gbuf[rows, :], wdn[rws(n * h, h), :], ROWS_BOTH, preferred_element_type=F32)

        pend["p", k] = [send(act_mine.at[rows], act_theirs.at[rows], other_c)]

    def activate(k):
        got(pend["p", k])

        @pl.loop(0, two // 16)
        def _(i):
            rows = rws(k * two + i * 16, 16)
            for n in range(2):
                def both(q):
                    at = (rows, pl.ds((q * 2 + n) * h, h))
                    return act_mine[at] + act_theirs[at]
                gate, up, grad = both(0), both(1), both(2)
                sig = jax.nn.sigmoid(gate)
                silu = gate * sig
                hid[rows, pl.ds(n * h, h)] = (silu * up).astype(BF)
                gact[rows, pl.ds(n * h, h)] = (grad * up * sig * (1.0 + gate * (1.0 - sig))).astype(BF)
                gact[rows, pl.ds((2 + n) * h, h)] = (grad * silu).astype(BF)

    def expand(k):
        rows = pl.ds(k * two, two)

        @pl.loop(0, 4)
        def _(n):
            at = lanes(n * 2 * f, 2 * f)
            pout[rows, at] = jnp.dot(hid[rows, :], wdn[:, at], preferred_element_type=F32).astype(BF)
            w = wgu[n].reshape(2 * f, 4 * h)
            pback[rows, at] = lax.dot_general(
                gact[rows, :], w, ROWS_BOTH, preferred_element_type=F32).astype(BF)

    def reduce_a(k, phase):
        mine, theirs, base = k * two + zl * cap, k * two + (1 - zl) * cap, k * two
        if phase == 1:
            at = lanes(off_a(xo, 0), 2 * f)
            pend["ra", k] = [send(pback.at[rws(base, cap), at], ax1.at[k, 0], right),
                             send(pback.at[rws(base + cap, cap), at], ax1.at[k, 1], left)]
        elif phase == 2:
            got(pend["ra", k])
            add_into(pback, base, cap, off_a(xr, 0), 2 * f, ax1.at[k, 0])
            add_into(pback, base + cap, cap, off_a(xl, 0), 2 * f, ax1.at[k, 1])
            pend["ra", k] = [send(pback.at[rws(base, two), lanes(off_a(xr, 0), 2 * f)], ax2.at[k, 0], right),
                             send(pback.at[rws(base, two), lanes(off_a(xl, 0), 2 * f)], ax2.at[k, 1], left)]
        elif phase == 3:
            got(pend["ra", k])
            add_into(pback, base, two, off_a(x, 0), 2 * f, ax2.at[k, 0], ax2.at[k, 1])
            pend["ra", k] = [send(pback.at[rws(theirs, cap), lanes(off_a(x, 0), 2 * f)], az.at[k], other_z)]
        elif phase == 4:
            got(pend["ra", k])
            add_into(pback, mine, cap, off_a(x, 0), 2 * f, az.at[k])
            pend["ra", k] = [send(pback.at[rws(mine, cap), lanes(off_a(x, 1 - yh), f)], ay.at[k], other_y)]
        else:
            got(pend["ra", k])
            add_into(pback, mine, cap, off_a(x, yh), f, ay.at[k])
            return_home(k, 1, pback, off_a(x, yh))

    def reduce_b(k, phase):
        mine, theirs, base = k * two + zl * cap, k * two + (1 - zl) * cap, k * two
        if phase == 1:
            pend["rb", k] = [send(pout.at[rws(base, two), lanes(off_b(1 - yh, 0), 4 * f)], by.at[k], other_y)]
        elif phase == 2:
            got(pend["rb", k])
            add_into(pout, base, two, off_b(yh, 0), 4 * f, by.at[k])
            at = lanes(off_b(yh, xo), f)
            pend["rb", k] = [send(pout.at[rws(base, cap), at], bx1.at[k, 0], right),
                             send(pout.at[rws(base + cap, cap), at], bx1.at[k, 1], left)]
        elif phase == 3:
            got(pend["rb", k])
            add_into(pout, base, cap, off_b(yh, xr), f, bx1.at[k, 0])
            add_into(pout, base + cap, cap, off_b(yh, xl), f, bx1.at[k, 1])
            pend["rb", k] = [send(pout.at[rws(base, two), lanes(off_b(yh, xr), f)], bx2.at[k, 0], right),
                             send(pout.at[rws(base, two), lanes(off_b(yh, xl), f)], bx2.at[k, 1], left)]
        elif phase == 4:
            got(pend["rb", k])
            add_into(pout, base, two, off_b(yh, x), f, bx2.at[k, 0], bx2.at[k, 1])
            pend["rb", k] = [send(pout.at[rws(theirs, cap), lanes(off_b(yh, x), f)], bz.at[k], other_z)]
        else:
            got(pend["rb", k])
            add_into(pout, mine, cap, off_b(yh, x), f, bz.at[k])
            return_home(k, 0, pout, off_b(yh, x))

    def return_home(k, a, buf, off):
        src = buf.at[rws(k * two + zl * cap, cap), lanes(off, f)]
        if k == 0:
            copy = pltpu.make_async_copy(src, home.at[a, 0], ls.at[8 + a])
            copy.start()
        else:
            copy = send(src, home.at[a, k], dev(**source(k)))
        pend["h", k, a] = copy

    def weight_grads():
        @pl.loop(0, 8)
        def _(p):
            xx, yy = p // 2, p % 2
            gwt[xx, yy] = lax.dot_general(
                tbuf[:, lanes(p * f, f)], gact[...], ROWS_TOP, preferred_element_type=F32).astype(BF)
            for q, out in enumerate((gg, gu)):
                pltpu.make_async_copy(
                    gwt.at[xx, yy, :, lanes(2 * h * q + h * c, h)], out.at[yy, xx, c], ls.at[10]).start()
                pltpu.make_async_remote_copy(
                    src_ref=gwt.at[xx, yy, :, lanes(2 * h * q + h * (1 - c), h)], dst_ref=out.at[yy, xx, c],
                    send_sem=ls.at[11], recv_sem=ls.at[12], device_id=other_c, device_id_type=MESH).start()

        @pl.loop(0, 8)
        def _(p):
            at = lanes(p * f, f)
            gdt[:, at] = lax.dot_general(
                hid[...], gbuf[:, at], ROWS_TOP, preferred_element_type=F32).astype(BF)
            there = lanes((p * 2 + c) * f, f)
            pltpu.make_async_copy(gdt.at[rws(h * c, h), at], gd.at[:, there], ls.at[13]).start()
            pltpu.make_async_remote_copy(
                src_ref=gdt.at[rws(h * (1 - c), h), at], dst_ref=gd.at[:, there],
                send_sem=ls.at[14], recv_sem=ls.at[15], device_id=other_c, device_id_type=MESH).start()

    def weight_grads_done():
        half_gu = gwt.at[:, :, :, pl.ds(0, 2 * h)]
        half_d = gdt.at[pl.ds(0, h)]
        for i, part in ((10, half_gu), (11, half_gu), (12, half_gu), (13, half_d), (14, half_d), (15, half_d)):
            pltpu.make_async_copy(part, part, ls.at[i]).wait()

    def gather(k, phase):
        gather_a(k, phase)
        gather_b(k, phase)

    for k in range(CHUNKS):
        dispatch(k)
    for k in range(CHUNKS):
        dispatched(k)
        gather(k, 1)
    gather(0, 2)
    gather(1, 2)
    gather(0, 3)
    gather(0, 4)
    gather(1, 3)
    gather(2, 2)
    weights_ready()
    for k in range(CHUNKS):
        gather(k, 5)
        if k + 1 < CHUNKS:
            gather(k + 1, 4)
        if k + 2 < CHUNKS:
            gather(k + 2, 3)
        if k + 3 < CHUNKS:
            gather(k + 3, 2)
        project(k)
        if k:
            reduce_a(k - 1, 2)
        activate(k)
        expand(k)
        reduce_a(k, 1)
        reduce_b(k, 1)
        if k:
            reduce_a(k - 1, 3)
            reduce_b(k - 1, 2)
    reduce_a(2, 4)
    reduce_b(2, 3)
    for k in (0, 1):
        reduce_a(k, 4)
        reduce_b(k, 3)
    reduce_a(3, 2)
    weight_grads()
    for k in (0, 1, 2):
        reduce_a(k, 5)
        reduce_b(k, 4)
    reduce_a(3, 3)
    reduce_b(3, 2)
    for k in (0, 1, 2):
        reduce_b(k, 5)
    reduce_a(3, 4)
    reduce_b(3, 3)
    reduce_a(3, 5)
    reduce_b(3, 4)
    reduce_b(3, 5)
    weight_grads_done()
    for a, out in ((1, gt), (0, lo)):
        total = jnp.zeros(out.shape, F32)
        for k in range(CHUNKS):
            if k == 0:
                pend["h", k, a].wait()
            else:
                pend["h", k, a].wait_recv()
            total = total + lax.dot_general(picks[1 - a, k], home[a, k], ROWS_TOP, preferred_element_type=F32)
        out[...] = total.astype(BF)
    for copy in started:
        copy.wait_send()


def body(tokens, grad_out, expert_ids, gate_num, gate_weight, up_weight, down_weight):
    count, f = tokens.shape
    d, h = gate_weight.shape
    cap = 5 * count // 8
    rows, d2 = 8 * cap, 8 * f
    meta = jnp.concatenate([expert_ids.T, gate_num[None, :], jnp.zeros((5, count), jnp.int32)], axis=0)
    split = (2, 4, 2, f, h)
    vm = pl.BlockSpec(memory_space=pltpu.VMEM)
    anywhere = pl.BlockSpec(memory_space=pl.ANY)

    def v(*shape, dtype=BF):
        return pltpu.VMEM(shape, dtype)

    sems = 112
    lo, gt, gg, gu, gd = pl.pallas_call(
        functools.partial(kernel, cap, f, h, None),
        out_shape=(
            jax.ShapeDtypeStruct((count, f), BF), jax.ShapeDtypeStruct((count, f), BF),
            jax.ShapeDtypeStruct(split, BF), jax.ShapeDtypeStruct(split, BF),
            jax.ShapeDtypeStruct((h, d), BF)),
        in_specs=[vm, vm, vm, anywhere, anywhere, anywhere],
        out_specs=(vm, vm, anywhere, anywhere, anywhere),
        scratch_shapes=[
            v(2, 4, cap, count), v(2, 4, cap, f), v(rows, d2), v(rows, d2),
            v(4, 2, f, 4 * h), v(2 * h, d2),
            v(rows, 6 * h, dtype=F32), v(rows, 6 * h, dtype=F32), v(rows, 2 * h), v(rows, 4 * h),
            v(rows, d2), v(rows, d2),
            v(4, 2, cap, 2 * f), v(4, 2, 2 * cap, 2 * f), v(4, cap, 2 * f), v(4, cap, f),
            v(4, 2 * cap, 4 * f), v(4, 2, cap, f), v(4, 2, 2 * cap, f), v(4, cap, f),
            v(2, 4, cap, f), v(4, 2, f, 4 * h), v(2 * h, d2),
            pltpu.SemaphoreType.DMA((sems,)), pltpu.SemaphoreType.DMA((sems,)), pltpu.SemaphoreType.DMA((16,)),
        ],
        compiler_params=pltpu.CompilerParams(
            collective_id=1, has_side_effects=True, vmem_limit_bytes=60 * 2**20),
        name="moe_layer",
    )(meta, tokens, grad_out, gate_weight.reshape(split), up_weight.reshape(split), down_weight)
    return lo, gt, gg.reshape(d, h), gu.reshape(d, h), gd


def solution(mesh):
    placed = (
        P("grp", "col"),
        P("grp", "col"),
        P("grp", None),
        P("grp"),
        P(None, ("grp", "col")),
        P(None, ("grp", "col")),
        P(("grp", "col"), None),
    )
    return jax.shard_map(
        body,
        mesh=mesh,
        in_specs=placed,
        out_specs=(
            P("grp", "col"),
            P("grp", "col"),
            P(None, ("grp", "col")),
            P(None, ("grp", "col")),
            P(("grp", "col"), None),
        ),
        check_vma=False,
    )
```

```python
import functools

import jax
import jax.numpy as jnp
from jax import lax
from jax.experimental import pallas as pl
from jax.experimental.pallas import tpu as pltpu
from jax.sharding import PartitionSpec as P

MESH = pl.DeviceIdType.MESH
BF = jnp.bfloat16
F32 = jnp.float32
CHUNKS = 4
ROWS_TOP = (((0,), (0,)), ((), ()))
ROWS_BOTH = (((1,), (1,)), ((), ()))
GATHER = (("zyx", "zyx", "yzx", "yzx"), ("xzy", "xyz", "xzy", "xyz"))
REDUCE = (("xzy", "xyz", "xzy", "zxy"), ("yzx", "yzx", "yxz", "zyx"))
ORDER = (
    "d11", "d21", "d31", "d20", "d10", "d00", "d30", "d01", "g001", "g011", "g111", "g211", "g002", "g101",
    "g012", "g311", "g112", "g201", "g102", "g212", "g301", "g013", "g003", "g312", "g202", "g113", "g213", "g103",
    "g302", "g014", "g004", "g313", "g203", "g114", "g104", "g214", "t0", "g303", "p0", "s0", "g204", "t1",
    "g314", "v0", "o0", "r001", "p1", "g304", "s1", "b0", "t2", "v1", "o1", "r101", "t3", "p2",
    "s2", "p3", "s3", "r011", "b1", "r111", "v2", "o2", "r201", "b2", "r211", "r112", "v3", "o3",
    "r301", "r102", "b3", "r311", "r002", "r012", "n0", "r113", "w0", "w2", "r312", "r202", "w1", "r212",
    "w3", "r013", "n2", "n1", "r003", "n3", "r114", "r313", "r302", "r213", "r004", "r303", "r203", "r103",
    "r214", "h11", "r014", "h00", "r314", "r304", "r204", "h21", "r104", "h01", "h31", "h30", "h20", "h10",
)


def boxes(cap, f):
    found = []
    for k in range(CHUNKS):
        for a in range(2):
            phase = 0
            for i in (2, 1, 0):
                axis, axes = REDUCE[a][k][i], REDUCE[a][k][:i]
                n = 2 * cap if "z" in axes else cap
                width = f * (4 if "x" in axes else 1) * (2 if "y" in axes else 1)
                phase += 1
                if axis == "x":
                    top = -(-n // 32) * 16
                    found += [((k, a, phase), (top, width)), ((k, a, phase), (n - top, width))]
                    phase += 1
                    found += [((k, a, phase), (n, width))] * 2
                else:
                    found.append(((k, a, phase), (n, width)))
    return found


def box_keys():
    return [key for key, _ in boxes(16, 128)]


def kernel(cap, f, h,
           meta, tok, gout, wg, wu, wd,
           lo, gt, gg, gu, gd,
           picks, sent, tbuf, gbuf, wgu, wdn, act_mine, act_theirs, hid, gact, pout, pback,
           home, gwt, gdt, ss, rs, ls, *landings):
    d2 = 8 * f
    grp, col = lax.axis_index("grp"), lax.axis_index("col")
    yl, z = grp // 4, grp % 4
    zh, zl = z // 2, z % 2
    yh, x, c = col // 8, (col // 2) % 4, col % 2
    xr, xl, xo = (x + 1) % 4, (x + 3) % 4, (x + 2) % 4

    def dev(yl=yl, z=z, yh=yh, x=x, c=c):
        return (yl * 4 + z, (yh * 4 + x) * 2 + c)

    right, left = dev(x=xr), dev(x=xl)
    other_y, other_z, other_c = dev(yh=1 - yh), dev(z=z + 1 - 2 * zl), dev(c=1 - c)

    def source(k):
        dy, dz = k // 2, k % 2
        return dict(yl=1 - yl if dy else yl, z=3 - z if dz else z)

    counter = [0]
    started = []
    inbox, landing = {}, {}
    for key, box in zip(box_keys(), landings):
        inbox.setdefault(key, []).append(box)

    def send(src, dst, target):
        i = counter[0]
        counter[0] += 1
        copy = pltpu.make_async_remote_copy(
            src_ref=src, dst_ref=dst, send_sem=ss.at[i], recv_sem=rs.at[i],
            device_id=target, device_id_type=MESH)
        copy.start()
        started.append(copy)
        return copy

    def got(copies):
        for copy in copies:
            copy.wait_recv()

    def lanes(off, n):
        return pl.ds(pl.multiple_of(off, 128), n)

    def rws(off, n):
        return pl.ds(pl.multiple_of(off, 16), n)

    def off_a(x, yh):
        return (x * 2 + yh) * f

    def off_b(yh, x):
        return (yh * 4 + x) * f

    def add_into(dst, row, n, off, width, *srcs):
        @pl.loop(0, n // 16)
        def _(i):
            at = (rws(row + i * 16, 16), lanes(off, width))
            total = dst[at].astype(F32)
            for src in srcs:
                total = total + src[rws(i * 16, 16), :].astype(F32)
            dst[at] = total.astype(BF)

    barrier = pltpu.get_barrier_semaphore()
    partners = [right, left, other_y, other_z, other_c] + [dev(**source(k)) for k in (1, 2, 3)]
    for partner in partners:
        pl.semaphore_signal(barrier, inc=1, device_id=partner, device_id_type=MESH)

    for y in range(2):
        for q, w in enumerate((wg, wu)):
            at = (slice(None), y, slice(None), lanes(2 * h * q + h * c, h))
            pltpu.make_async_copy(w.at[y, :, c], wgu.at[at], ls.at[0]).start()
    for p in range(8):
        at = (rws(h * c, h), pl.ds(p * f, f))
        pltpu.make_async_copy(wd.at[:, lanes((p * 2 + c) * f, f)], wdn.at[at], ls.at[3]).start()

    def weights_from_other():
        for y in range(2):
            for q, w in enumerate((wg, wu)):
                at = (slice(None), y, slice(None), lanes(2 * h * q + h * c, h))
                pltpu.make_async_remote_copy(
                    src_ref=w.at[y, :, 1 - c], dst_ref=wgu.at[at], send_sem=ls.at[1], recv_sem=ls.at[2],
                    device_id=other_c, device_id_type=MESH).start()
        for p in range(8):
            at = (rws(h * c, h), pl.ds(p * f, f))
            pltpu.make_async_remote_copy(
                src_ref=wd.at[:, lanes((p * 2 + 1 - c) * f, f)], dst_ref=wdn.at[at], send_sem=ls.at[4],
                recv_sem=ls.at[5], device_id=other_c, device_id_type=MESH).start()

    ready = []

    def weights_ready():
        half_gu = wgu.at[:, :, :, pl.ds(0, 2 * h)]
        half_d = wdn.at[pl.ds(0, h)]
        for i, part in ((0, half_gu), (1, half_gu), (2, half_gu), (3, half_d), (4, half_d), (5, half_d)):
            pltpu.make_async_copy(part, part, ls.at[i]).wait()

    first, second = meta[0:1, :], meta[1:2, :]
    share = meta[2:3, :].astype(F32) / 64.0
    count = first.shape[1]
    has, weight = [], []
    for k in range(CHUNKS):
        where = source(k)
        expert = where["yl"] * 2 + where["z"] // 2
        one, two = first == expert, second == expert
        has.append(jnp.logical_or(one, two).astype(F32))
        weight.append(jnp.where(one, share, 1.0 - share))
    marks = jnp.concatenate(has + [jnp.zeros((4, count), F32)], axis=0)
    before = (lax.broadcasted_iota(jnp.int32, (count, count), 0)
              < lax.broadcasted_iota(jnp.int32, (count, count), 1)).astype(F32)
    position = jnp.dot(marks.astype(BF), before.astype(BF), preferred_element_type=F32)
    slot = lax.broadcasted_iota(jnp.int32, (cap, count), 0).astype(F32)
    for k in range(CHUNKS):
        chosen = jnp.where(slot == position[k:k + 1, :], has[k], 0.0)
        picks[0, k] = chosen.astype(BF)
        picks[1, k] = (chosen * weight[k]).astype(BF)
        sent[0, k] = jnp.dot(picks[0, k], tok[...], preferred_element_type=F32).astype(BF)
        sent[1, k] = jnp.dot(picks[1, k], gout[...], preferred_element_type=F32).astype(BF)

    pend = {}
    two = 2 * cap
    bufs = (tbuf, gbuf)
    sums = (pout, pback)

    def region(tokens_first, k, axes, z=zl, x=x, y=yh):
        row, n = (k * two, two) if "z" in axes else (k * two + z * cap, cap)
        if "x" in axes and "y" in axes:
            off, width = 0, d2
        elif tokens_first:
            off, width = (off_a(x, 0), 2 * f) if "y" in axes else (off_a(x, y), f)
        else:
            off, width = (off_b(y, 0), 4 * f) if "x" in axes else (off_b(y, x), f)
        return row, n, off, width

    def view(buf, part):
        row, n, off, width = part
        return buf.at[rws(row, n), lanes(off, width)]

    def halves(part):
        row, n, off, width = part
        top = -(-n // 32) * 16
        return (row, top, off, width), (row + top, n - top, off, width)

    def dispatch(k, a):
        off = (off_a(x, yh), off_b(yh, x))[a]
        theirs = 1 - zl if k % 2 else zl
        dst = bufs[a].at[rws(k * two + theirs * cap, cap), lanes(off, f)]
        if k == 0:
            copy = pltpu.make_async_copy(sent.at[a, 0], dst, ls.at[6 + a])
            copy.start()
            pend["g", k, a] = [copy]
        else:
            pend["g", k, a] = [send(sent.at[a, k], dst, dev(**source(k)))]

    def gathered(k, a, phase):
        if phase == 0 and k == 0:
            pend["g", k, a][0].wait()
        else:
            got(pend["g", k, a])

    def gather(k, a, phase):
        gathered(k, a, phase - 1)
        steps = []
        for i, axis in enumerate(GATHER[a][k]):
            steps += [(axis, i, 0), (axis, i, 1)] if axis == "x" else [(axis, i, 0)]
        axis, i, later = steps[phase - 1]
        buf, axes = bufs[a], GATHER[a][k][:i]
        if axis == "x" and later:
            up = view(buf, halves(region(a == 0, k, axes, x=xl))[0])
            down = view(buf, halves(region(a == 0, k, axes, x=xr))[1])
            pend["g", k, a] = [send(up, up, right), send(down, down, left)]
        else:
            mine = view(buf, region(a == 0, k, axes))
            to = (right, left) if axis == "x" else (other_y,) if axis == "y" else (other_z,)
            pend["g", k, a] = [send(mine, mine, target) for target in to]

    def project_tokens(k):
        gathered(k, 0, 4)
        rows = pl.ds(k * two, two)
        if not ready:
            weights_ready()
            ready.append(True)

        @pl.loop(0, 2)
        def _(n):
            w = wgu[:, :, :, lanes(n * 2 * h, 2 * h)].reshape(d2, 2 * h)
            act_mine[rows, lanes(n * 2 * h, 2 * h)] = jnp.dot(tbuf[rows, :], w, preferred_element_type=F32)

    def project_grads(k):
        gathered(k, 1, 4)
        rows = pl.ds(k * two, two)
        if not ready:
            weights_ready()
            ready.append(True)

        @pl.loop(0, 2)
        def _(n):
            act_mine[rows, lanes((4 + n) * h, h)] = lax.dot_general(
                gbuf[rows, :], wdn[rws(n * h, h), :], ROWS_BOTH, preferred_element_type=F32)

    def swap(k):
        rows = pl.ds(k * two, two)
        pend["p", k] = [send(act_mine.at[rows], act_theirs.at[rows], other_c)]

    def activate(k):
        got(pend["p", k])

        @pl.loop(0, two // 16)
        def _(i):
            rows = rws(k * two + i * 16, 16)
            for n in range(2):
                def both(q):
                    at = (rows, pl.ds((q * 2 + n) * h, h))
                    return act_mine[at] + act_theirs[at]
                gate, up, grad = both(0), both(1), both(2)
                sig = jax.nn.sigmoid(gate)
                silu = gate * sig
                hid[rows, pl.ds(n * h, h)] = (silu * up).astype(BF)
                gact[rows, pl.ds(n * h, h)] = (grad * up * sig * (1.0 + gate * (1.0 - sig))).astype(BF)
                gact[rows, pl.ds((2 + n) * h, h)] = (grad * silu).astype(BF)

    def expand_out(k):
        rows = pl.ds(k * two, two)

        @pl.loop(0, 4)
        def _(n):
            at = lanes(n * 2 * f, 2 * f)
            pout[rows, at] = jnp.dot(hid[rows, :], wdn[:, at], preferred_element_type=F32).astype(BF)

    def expand_back(k):
        rows = pl.ds(k * two, two)

        @pl.loop(0, 4)
        def _(n):
            w = wgu[n].reshape(2 * f, 4 * h)
            pback[rows, lanes(n * 2 * f, 2 * f)] = lax.dot_general(
                gact[rows, :], w, ROWS_BOTH, preferred_element_type=F32).astype(BF)

    def swap_in(k, a, landed):
        got(pend["r", k, a])
        for part, slots in landed:
            row, n, off, width = part
            add_into(sums[a], row, n, off, width, *slots)

    def reduce(k, a, phase):
        steps = []
        for i in (2, 1, 0):
            axis = REDUCE[a][k][i]
            steps += [(axis, i, 0), (axis, i, 1)] if axis == "x" else [(axis, i, 0)]
        if phase > 1:
            swap_in(k, a, landing[k, a])
        axis, i, later = steps[phase - 1]
        first_x, axes = a == 1, REDUCE[a][k][:i]
        place = functools.partial(region, first_x, k, axes)
        if axis == "x":
            up, down = place(x=xr if later else xo), place(x=xl if later else xo)
            if not later:
                up, down = halves(up)[0], halves(down)[1]
            moves = [(up, right), (down, left)]
            if later:
                added = [(place(), (0, 1))]
            else:
                added = [(halves(place(x=xr))[0], (0,)), (halves(place(x=xl))[1], (1,))]
        elif axis == "y":
            moves, added = [(place(y=1 - yh), other_y)], [(place(), (0,))]
        else:
            moves, added = [(place(z=1 - zl), other_z)], [(place(), (0,))]
        slots = inbox[k, a, phase]
        pend["r", k, a] = [send(view(sums[a], part), slot, target) for (part, target), slot in zip(moves, slots)]
        landing[k, a] = [(part, [slots[j] for j in which]) for part, which in added]

    def return_home(k, a):
        swap_in(k, a, landing[k, a])
        src = view(sums[a], region(a == 1, k, ""))
        if k == 0:
            copy = pltpu.make_async_copy(src, home.at[a, 0], ls.at[8 + a])
            copy.start()
        else:
            copy = send(src, home.at[a, k], dev(**source(k)))
        pend["h", k, a] = copy

    def weight_grads_up(part):
        @pl.loop(part * 2, part * 2 + 2)
        def _(p):
            xx, yy = p // 2, p % 2
            gwt[xx, yy] = lax.dot_general(
                tbuf[:, lanes(p * f, f)], gact[...], ROWS_TOP, preferred_element_type=F32).astype(BF)
            for q, out in enumerate((gg, gu)):
                pltpu.make_async_copy(
                    gwt.at[xx, yy, :, lanes(2 * h * q + h * c, h)], out.at[yy, xx, c], ls.at[10]).start()
                pltpu.make_async_remote_copy(
                    src_ref=gwt.at[xx, yy, :, lanes(2 * h * q + h * (1 - c), h)], dst_ref=out.at[yy, xx, c],
                    send_sem=ls.at[11], recv_sem=ls.at[12], device_id=other_c, device_id_type=MESH).start()

    def weight_grads_down(part):
        @pl.loop(part * 2, part * 2 + 2)
        def _(p):
            at = lanes(p * f, f)
            gdt[:, at] = lax.dot_general(
                hid[...], gbuf[:, at], ROWS_TOP, preferred_element_type=F32).astype(BF)
            there = lanes((p * 2 + c) * f, f)
            pltpu.make_async_copy(gdt.at[rws(h * c, h), at], gd.at[:, there], ls.at[13]).start()
            pltpu.make_async_remote_copy(
                src_ref=gdt.at[rws(h * (1 - c), h), at], dst_ref=gd.at[:, there],
                send_sem=ls.at[14], recv_sem=ls.at[15], device_id=other_c, device_id_type=MESH).start()

    def weight_grads_done():
        half_gu = gwt.at[:, :, :, pl.ds(0, 2 * h)]
        half_d = gdt.at[pl.ds(0, h)]
        for i, part in ((10, half_gu), (11, half_gu), (12, half_gu), (13, half_d), (14, half_d), (15, half_d)):
            pltpu.make_async_copy(part, part, ls.at[i]).wait()

    steps = dict(d=dispatch, g=gather, t=project_tokens, p=project_grads, s=swap, v=activate, o=expand_out,
                 b=expand_back, r=reduce, h=return_home, w=weight_grads_up, n=weight_grads_down)
    pl.semaphore_wait(barrier, len(partners))
    weights_from_other()
    for step in ORDER:
        steps[step[0]](*(int(digit) for digit in step[1:]))
    weight_grads_done()
    for a, out in ((1, gt), (0, lo)):
        total = jnp.zeros(out.shape, F32)
        for k in range(CHUNKS):
            if k == 0:
                pend["h", k, a].wait()
            else:
                pend["h", k, a].wait_recv()
            total = total + lax.dot_general(picks[1 - a, k], home[a, k], ROWS_TOP, preferred_element_type=F32)
        out[...] = total.astype(BF)
    for copy in started:
        copy.wait_send()


def body(tokens, grad_out, expert_ids, gate_num, gate_weight, up_weight, down_weight):
    count, f = tokens.shape
    d, h = gate_weight.shape
    cap = 5 * count // 8
    rows, d2 = 8 * cap, 8 * f
    meta = jnp.concatenate([expert_ids.T, gate_num[None, :], jnp.zeros((5, count), jnp.int32)], axis=0)
    split = (2, 4, 2, f, h)
    vm = pl.BlockSpec(memory_space=pltpu.VMEM)
    anywhere = pl.BlockSpec(memory_space=pl.ANY)

    def v(*shape, dtype=BF):
        return pltpu.VMEM(shape, dtype)

    sems = 112
    lo, gt, gg, gu, gd = pl.pallas_call(
        functools.partial(kernel, cap, f, h),
        out_shape=(
            jax.ShapeDtypeStruct((count, f), BF), jax.ShapeDtypeStruct((count, f), BF),
            jax.ShapeDtypeStruct(split, BF), jax.ShapeDtypeStruct(split, BF),
            jax.ShapeDtypeStruct((h, d), BF)),
        in_specs=[vm, vm, vm, anywhere, anywhere, anywhere],
        out_specs=(vm, vm, anywhere, anywhere, anywhere),
        scratch_shapes=[
            v(2, 4, cap, count), v(2, 4, cap, f), v(rows, d2), v(rows, d2),
            v(4, 2, f, 4 * h), v(2 * h, d2),
            v(rows, 6 * h, dtype=F32), v(rows, 6 * h, dtype=F32), v(rows, 2 * h), v(rows, 4 * h),
            v(rows, d2), v(rows, d2),
            v(2, 4, cap, f), v(4, 2, f, 4 * h), v(2 * h, d2),
            pltpu.SemaphoreType.DMA((sems,)), pltpu.SemaphoreType.DMA((sems,)), pltpu.SemaphoreType.DMA((16,)),
        ] + [v(*shape) for _, shape in boxes(cap, f)],
        compiler_params=pltpu.CompilerParams(
            collective_id=1, has_side_effects=True, vmem_limit_bytes=60 * 2**20),
        name="moe_layer",
    )(meta, tokens, grad_out, gate_weight.reshape(split), up_weight.reshape(split), down_weight)
    return lo, gt, gg.reshape(d, h), gu.reshape(d, h), gd


def solution(mesh):
    placed = (
        P("grp", "col"),
        P("grp", "col"),
        P("grp", None),
        P("grp"),
        P(None, ("grp", "col")),
        P(None, ("grp", "col")),
        P(("grp", "col"), None),
    )
    return jax.shard_map(
        body,
        mesh=mesh,
        in_specs=placed,
        out_specs=(
            P("grp", "col"),
            P("grp", "col"),
            P(None, ("grp", "col")),
            P(None, ("grp", "col")),
            P(("grp", "col"), None),
        ),
        check_vma=False,
    )
```

```python
import functools

import jax
import jax.numpy as jnp
from jax import lax
from jax.experimental import pallas as pl
from jax.experimental.pallas import tpu as pltpu
from jax.sharding import PartitionSpec as P

MESH = pl.DeviceIdType.MESH
BF = jnp.bfloat16
F32 = jnp.float32
CHUNKS = 4
ROWS_TOP = (((0,), (0,)), ((), ()))
ROWS_BOTH = (((1,), (1,)), ((), ()))
GATHER = (("zyx", "yzx", "zyx", "yzx"), ("xzy", "xyz", "xyz", "xzy"))
REDUCE = (("zxy", "xzy", "xyz", "xyz"), ("yzx", "zyx", "yzx", "yzx"))
ORDER = (
    "d31", "d00", "d01", "d21", "g001", "d20", "d10", "d11", "g011", "d30", "g311", "g002", "g101", "g211",
    "g012", "g111", "g201", "g312", "g301", "g212", "g013", "g202", "g003", "g112", "g102", "g313", "g213", "g302",
    "g203", "g014", "g004", "g113", "g103", "g214", "g204", "g314", "t0", "g303", "p0", "s0", "g104", "t2",
    "g114", "v0", "b0", "g304", "p2", "r011", "s2", "o0", "t1", "r001", "t3", "v2", "o2", "r201",
    "r012", "p3", "s3", "p1", "s1", "b2", "r211", "v3", "b3", "r311", "v1", "r013", "o1", "r101",
    "r212", "o3", "r301", "r202", "b1", "r111", "r312", "r014", "r002", "w0", "r213", "n1", "n2", "r112",
    "w2", "r102", "n0", "r302", "w3", "r313", "r214", "r003", "n3", "r203", "h01", "w1", "r113", "r103",
    "r303", "r314", "r004", "r204", "h21", "r104", "r304", "r114", "h00", "h20", "h31", "h10", "h30", "h11",
)


def boxes(cap, f):
    found = []
    for k in range(CHUNKS):
        for a in range(2):
            phase = 0
            for i in (2, 1, 0):
                axis, axes = REDUCE[a][k][i], REDUCE[a][k][:i]
                n = 2 * cap if "z" in axes else cap
                width = f * (4 if "x" in axes else 1) * (2 if "y" in axes else 1)
                phase += 1
                if axis == "x":
                    top = -(-n // 32) * 16
                    found += [((k, a, phase), (top, width)), ((k, a, phase), (n - top, width))]
                    phase += 1
                    found += [((k, a, phase), (n, width))] * 2
                else:
                    found.append(((k, a, phase), (n, width)))
    return found


def box_keys():
    return [key for key, _ in boxes(16, 128)]


def place():
    grp, col = lax.axis_index("grp"), lax.axis_index("col")
    return grp // 4, grp % 4, col // 8, (col // 2) % 4, col % 2


def sources(yl, z):
    return [dict(yl=1 - yl if k // 2 else yl, z=3 - z if k % 2 else z) for k in range(CHUNKS)]


def routing(cap, ids, nums, yl, z):
    first, second = ids[0:1, :], ids[1:2, :]
    share = nums[...].astype(F32) / 64.0
    count = first.shape[1]
    has, weight = [], []
    for where in sources(yl, z):
        expert = where["yl"] * 2 + where["z"] // 2
        one, two = first == expert, second == expert
        has.append(jnp.logical_or(one, two).astype(F32))
        weight.append(jnp.where(one, share, 1.0 - share))
    marks = jnp.concatenate(has + [jnp.zeros((4, count), F32)], axis=0)
    before = (lax.broadcasted_iota(jnp.int32, (count, count), 0)
              < lax.broadcasted_iota(jnp.int32, (count, count), 1)).astype(F32)
    position = jnp.dot(marks.astype(BF), before.astype(BF), preferred_element_type=F32)
    slot = lax.broadcasted_iota(jnp.int32, (cap, count), 0).astype(F32)
    found = []
    for k in range(CHUNKS):
        chosen = jnp.where(slot == position[k:k + 1, :], has[k], 0.0)
        found.append((chosen.astype(BF), (chosen * weight[k]).astype(BF)))
    return found


def finish(cap, parts, ids, nums, home, gg, gu, gd, lo, gt, ggo, guo, gdo, tall, wide, into, out_of):
    long, across = gg.shape[0] // parts, gd.shape[1] // parts
    ins, outs = [], []
    for i in range(parts):
        rows, lanes = (pl.ds(i * long, long), slice(None)), (slice(None), pl.ds(i * across, across))
        for q, (src, held, dst, at) in enumerate((
                (gg, tall.at[0], ggo, rows), (gu, tall.at[1], guo, rows), (gd, wide, gdo, lanes))):
            ins.append(pltpu.make_async_copy(src.at[at], held.at[at], into.at[q, i]))
            outs.append(pltpu.make_async_copy(held.at[at], dst.at[at], out_of.at[q, i]))
    for copy in ins:
        copy.start()
    for landed, leaving in zip(ins, outs):
        landed.wait()
        leaving.start()
    yl, z, _, _, _ = place()
    picks = routing(cap, ids, nums, yl, z)
    for a, out in ((0, lo), (1, gt)):
        total = jnp.zeros(out.shape, F32)
        for k in range(CHUNKS):
            total = total + lax.dot_general(picks[k][1 - a], home[a, k], ROWS_TOP, preferred_element_type=F32)
        out[...] = total.astype(BF)
    for copy in outs:
        copy.wait()


def kernel(cap, f, h,
           ids, nums, tok, gout, wg, wu, wd,
           home, gg, gu, gd,
           sent, tbuf, gbuf, wgu, wdn, act_mine, act_theirs, hid, gact, pout, pback,
           gwt, gdt, ss, rs, ls, *landings):
    d2 = 8 * f
    yl, z, yh, x, c = place()
    zl = z % 2
    xr, xl, xo = (x + 1) % 4, (x + 3) % 4, (x + 2) % 4

    def dev(yl=yl, z=z, yh=yh, x=x, c=c):
        return (yl * 4 + z, (yh * 4 + x) * 2 + c)

    right, left = dev(x=xr), dev(x=xl)
    other_y, other_z, other_c = dev(yh=1 - yh), dev(z=z + 1 - 2 * zl), dev(c=1 - c)

    homes = sources(yl, z)

    counter = [0]
    started = []
    inbox, landing = {}, {}
    for key, box in zip(box_keys(), landings):
        inbox.setdefault(key, []).append(box)

    def send(src, dst, target):
        i = counter[0]
        counter[0] += 1
        copy = pltpu.make_async_remote_copy(
            src_ref=src, dst_ref=dst, send_sem=ss.at[i], recv_sem=rs.at[i],
            device_id=target, device_id_type=MESH)
        copy.start()
        started.append(copy)
        return copy

    def got(copies):
        for copy in copies:
            copy.wait_recv()

    def lanes(off, n):
        return pl.ds(pl.multiple_of(off, 128), n)

    def rws(off, n):
        return pl.ds(pl.multiple_of(off, 16), n)

    def off_a(x, yh):
        return (x * 2 + yh) * f

    def off_b(yh, x):
        return (yh * 4 + x) * f

    def add_into(dst, row, n, off, width, *srcs):
        @pl.loop(0, n // 16)
        def _(i):
            at = (rws(row + i * 16, 16), lanes(off, width))
            total = dst[at].astype(F32)
            for src in srcs:
                total = total + src[rws(i * 16, 16), :].astype(F32)
            dst[at] = total.astype(BF)

    barrier = pltpu.get_barrier_semaphore()
    partners = [right, left, other_y, other_z, other_c] + [dev(**homes[k]) for k in (1, 2, 3)]
    for partner in partners:
        pl.semaphore_signal(barrier, inc=1, device_id=partner, device_id_type=MESH)

    for y in range(2):
        for q, w in enumerate((wg, wu)):
            at = (slice(None), y, slice(None), lanes(2 * h * q + h * c, h))
            pltpu.make_async_copy(w.at[y, :, c], wgu.at[at], ls.at[0]).start()
    for p in range(8):
        at = (rws(h * c, h), pl.ds(p * f, f))
        pltpu.make_async_copy(wd.at[:, lanes((p * 2 + c) * f, f)], wdn.at[at], ls.at[3]).start()

    def weights_from_other():
        for y in range(2):
            for q, w in enumerate((wg, wu)):
                at = (slice(None), y, slice(None), lanes(2 * h * q + h * c, h))
                pltpu.make_async_remote_copy(
                    src_ref=w.at[y, :, 1 - c], dst_ref=wgu.at[at], send_sem=ls.at[1], recv_sem=ls.at[2],
                    device_id=other_c, device_id_type=MESH).start()
        for p in range(8):
            at = (rws(h * c, h), pl.ds(p * f, f))
            pltpu.make_async_remote_copy(
                src_ref=wd.at[:, lanes((p * 2 + 1 - c) * f, f)], dst_ref=wdn.at[at], send_sem=ls.at[4],
                recv_sem=ls.at[5], device_id=other_c, device_id_type=MESH).start()

    ready = []

    def weights_ready():
        half_gu = wgu.at[:, :, :, pl.ds(0, 2 * h)]
        half_d = wdn.at[pl.ds(0, h)]
        for i, part in ((0, half_gu), (1, half_gu), (2, half_gu), (3, half_d), (4, half_d), (5, half_d)):
            pltpu.make_async_copy(part, part, ls.at[i]).wait()

    picks = routing(cap, ids, nums, yl, z)
    pend = {}
    two = 2 * cap
    bufs = (tbuf, gbuf)
    sums = (pout, pback)

    def region(tokens_first, k, axes, z=zl, x=x, y=yh):
        row, n = (k * two, two) if "z" in axes else (k * two + z * cap, cap)
        if "x" in axes and "y" in axes:
            off, width = 0, d2
        elif tokens_first:
            off, width = (off_a(x, 0), 2 * f) if "y" in axes else (off_a(x, y), f)
        else:
            off, width = (off_b(y, 0), 4 * f) if "x" in axes else (off_b(y, x), f)
        return row, n, off, width

    def view(buf, part):
        row, n, off, width = part
        return buf.at[rws(row, n), lanes(off, width)]

    def halves(part):
        row, n, off, width = part
        top = -(-n // 32) * 16
        return (row, top, off, width), (row + top, n - top, off, width)

    def dispatch(k, a):
        off = (off_a(x, yh), off_b(yh, x))[a]
        theirs = 1 - zl if k % 2 else zl
        sent[a, k] = jnp.dot(picks[k][a], (tok, gout)[a][...], preferred_element_type=F32).astype(BF)
        dst = bufs[a].at[rws(k * two + theirs * cap, cap), lanes(off, f)]
        if k == 0:
            copy = pltpu.make_async_copy(sent.at[a, 0], dst, ls.at[6 + a])
            copy.start()
            pend["g", k, a] = [copy]
        else:
            pend["g", k, a] = [send(sent.at[a, k], dst, dev(**homes[k]))]

    def gathered(k, a, phase):
        if phase == 0 and k == 0:
            pend["g", k, a][0].wait()
        else:
            got(pend["g", k, a])

    def gather(k, a, phase):
        gathered(k, a, phase - 1)
        steps = []
        for i, axis in enumerate(GATHER[a][k]):
            steps += [(axis, i, 0), (axis, i, 1)] if axis == "x" else [(axis, i, 0)]
        axis, i, later = steps[phase - 1]
        buf, axes = bufs[a], GATHER[a][k][:i]
        if axis == "x" and later:
            up = view(buf, halves(region(a == 0, k, axes, x=xl))[0])
            down = view(buf, halves(region(a == 0, k, axes, x=xr))[1])
            pend["g", k, a] = [send(up, up, right), send(down, down, left)]
        else:
            mine = view(buf, region(a == 0, k, axes))
            to = (right, left) if axis == "x" else (other_y,) if axis == "y" else (other_z,)
            pend["g", k, a] = [send(mine, mine, target) for target in to]

    def project_tokens(k):
        gathered(k, 0, 4)
        rows = pl.ds(k * two, two)
        if not ready:
            weights_ready()
            ready.append(True)

        @pl.loop(0, 2)
        def _(n):
            w = wgu[:, :, :, lanes(n * 2 * h, 2 * h)].reshape(d2, 2 * h)
            act_mine[rows, lanes(n * 2 * h, 2 * h)] = jnp.dot(tbuf[rows, :], w, preferred_element_type=F32)

    def project_grads(k):
        gathered(k, 1, 4)
        rows = pl.ds(k * two, two)
        if not ready:
            weights_ready()
            ready.append(True)

        @pl.loop(0, 2)
        def _(n):
            act_mine[rows, lanes((4 + n) * h, h)] = lax.dot_general(
                gbuf[rows, :], wdn[rws(n * h, h), :], ROWS_BOTH, preferred_element_type=F32)

    def swap(k):
        rows = pl.ds(k * two, two)
        pend["p", k] = [send(act_mine.at[rows], act_theirs.at[rows], other_c)]

    def activate(k):
        got(pend["p", k])

        @pl.loop(0, two // 16)
        def _(i):
            rows = rws(k * two + i * 16, 16)
            for n in range(2):
                def both(q):
                    at = (rows, pl.ds((q * 2 + n) * h, h))
                    return act_mine[at] + act_theirs[at]
                gate, up, grad = both(0), both(1), both(2)
                sig = jax.nn.sigmoid(gate)
                silu = gate * sig
                hid[rows, pl.ds(n * h, h)] = (silu * up).astype(BF)
                gact[rows, pl.ds(n * h, h)] = (grad * up * sig * (1.0 + gate * (1.0 - sig))).astype(BF)
                gact[rows, pl.ds((2 + n) * h, h)] = (grad * silu).astype(BF)

    def expand_out(k):
        rows = pl.ds(k * two, two)

        @pl.loop(0, 4)
        def _(n):
            at = lanes(n * 2 * f, 2 * f)
            pout[rows, at] = jnp.dot(hid[rows, :], wdn[:, at], preferred_element_type=F32).astype(BF)

    def expand_back(k):
        rows = pl.ds(k * two, two)

        @pl.loop(0, 4)
        def _(n):
            w = wgu[n].reshape(2 * f, 4 * h)
            pback[rows, lanes(n * 2 * f, 2 * f)] = lax.dot_general(
                gact[rows, :], w, ROWS_BOTH, preferred_element_type=F32).astype(BF)

    def swap_in(k, a, landed):
        got(pend["r", k, a])
        for part, slots in landed:
            row, n, off, width = part
            add_into(sums[a], row, n, off, width, *slots)

    def reduce(k, a, phase):
        steps = []
        for i in (2, 1, 0):
            axis = REDUCE[a][k][i]
            steps += [(axis, i, 0), (axis, i, 1)] if axis == "x" else [(axis, i, 0)]
        if phase > 1:
            swap_in(k, a, landing[k, a])
        axis, i, later = steps[phase - 1]
        first_x, axes = a == 1, REDUCE[a][k][:i]
        spot = functools.partial(region, first_x, k, axes)
        if axis == "x":
            up, down = spot(x=xr if later else xo), spot(x=xl if later else xo)
            if not later:
                up, down = halves(up)[0], halves(down)[1]
            moves = [(up, right), (down, left)]
            if later:
                added = [(spot(), (0, 1))]
            else:
                added = [(halves(spot(x=xr))[0], (0,)), (halves(spot(x=xl))[1], (1,))]
        elif axis == "y":
            moves, added = [(spot(y=1 - yh), other_y)], [(spot(), (0,))]
        else:
            moves, added = [(spot(z=1 - zl), other_z)], [(spot(), (0,))]
        slots = inbox[k, a, phase]
        pend["r", k, a] = [send(view(sums[a], part), slot, target) for (part, target), slot in zip(moves, slots)]
        landing[k, a] = [(part, [slots[j] for j in which]) for part, which in added]

    def return_home(k, a):
        swap_in(k, a, landing[k, a])
        src = view(sums[a], region(a == 1, k, ""))
        if k == 0:
            copy = pltpu.make_async_copy(src, home.at[a, 0], ls.at[8 + a])
            copy.start()
        else:
            copy = send(src, home.at[a, k], dev(**homes[k]))
        pend["h", k, a] = copy

    def weight_grads_up(part):
        @pl.loop(part * 2, part * 2 + 2)
        def _(p):
            xx, yy = p // 2, p % 2
            gwt[xx, yy] = lax.dot_general(
                tbuf[:, lanes(p * f, f)], gact[...], ROWS_TOP, preferred_element_type=F32).astype(BF)
            for q, out in enumerate((gg, gu)):
                pltpu.make_async_copy(
                    gwt.at[xx, yy, :, lanes(2 * h * q + h * c, h)], out.at[yy, xx, c], ls.at[10]).start()
                pltpu.make_async_remote_copy(
                    src_ref=gwt.at[xx, yy, :, lanes(2 * h * q + h * (1 - c), h)], dst_ref=out.at[yy, xx, c],
                    send_sem=ls.at[11], recv_sem=ls.at[12], device_id=other_c, device_id_type=MESH).start()

    def weight_grads_down(part):
        @pl.loop(part * 2, part * 2 + 2)
        def _(p):
            at = lanes(p * f, f)
            gdt[:, at] = lax.dot_general(
                hid[...], gbuf[:, at], ROWS_TOP, preferred_element_type=F32).astype(BF)
            there = lanes((p * 2 + c) * f, f)
            pltpu.make_async_copy(gdt.at[rws(h * c, h), at], gd.at[:, there], ls.at[13]).start()
            pltpu.make_async_remote_copy(
                src_ref=gdt.at[rws(h * (1 - c), h), at], dst_ref=gd.at[:, there],
                send_sem=ls.at[14], recv_sem=ls.at[15], device_id=other_c, device_id_type=MESH).start()

    def weight_grads_done():
        half_gu = gwt.at[:, :, :, pl.ds(0, 2 * h)]
        half_d = gdt.at[pl.ds(0, h)]
        for i, part in ((10, half_gu), (11, half_gu), (12, half_gu), (13, half_d), (14, half_d), (15, half_d)):
            pltpu.make_async_copy(part, part, ls.at[i]).wait()

    steps = dict(d=dispatch, g=gather, t=project_tokens, p=project_grads, s=swap, v=activate, o=expand_out,
                 b=expand_back, r=reduce, h=return_home, w=weight_grads_up, n=weight_grads_down)
    pl.semaphore_wait(barrier, len(partners))
    drained = 0
    for i, step in enumerate(ORDER):
        steps[step[0]](*(int(digit) for digit in step[1:]))
        if i == 11:
            weights_from_other()
        old = max(len(started) - 40, 0)
        for copy in started[drained:old]:
            copy.wait_send()
        drained = old
    weight_grads_done()
    for copy in started[drained:]:
        copy.wait_send()
    for k in range(CHUNKS):
        for a in range(2):
            if k == 0:
                pend["h", k, a].wait()
            else:
                pend["h", k, a].wait_recv()


def body(tokens, grad_out, expert_ids, gate_num, gate_weight, up_weight, down_weight):
    count, f = tokens.shape
    d, h = gate_weight.shape
    cap = 5 * count // 8
    rows, d2 = 8 * cap, 8 * f
    ids, nums = expert_ids.T, gate_num.reshape(1, count)
    split = (2, 4, 2, f, h)
    vm = pl.BlockSpec(memory_space=pltpu.VMEM)
    anywhere = pl.BlockSpec(memory_space=pl.ANY)

    def v(*shape, dtype=BF):
        return pltpu.VMEM(shape, dtype)

    def like(*shape):
        return jax.ShapeDtypeStruct(shape, BF)

    sems = 112
    home, gg, gu, gd = pl.pallas_call(
        functools.partial(kernel, cap, f, h),
        out_shape=(like(2, CHUNKS, cap, f), like(*split), like(*split), like(h, d)),
        in_specs=[vm, vm, vm, vm, anywhere, anywhere, anywhere],
        out_specs=(anywhere, anywhere, anywhere, anywhere),
        scratch_shapes=[
            v(2, CHUNKS, cap, f), v(rows, d2), v(rows, d2),
            v(4, 2, f, 4 * h), v(2 * h, d2),
            v(rows, 6 * h, dtype=F32), v(rows, 6 * h, dtype=F32), v(rows, 2 * h), v(rows, 4 * h),
            v(rows, d2), v(rows, d2),
            v(4, 2, f, 4 * h), v(2 * h, d2),
            pltpu.SemaphoreType.DMA((sems,)), pltpu.SemaphoreType.DMA((sems,)), pltpu.SemaphoreType.DMA((16,)),
        ] + [v(*shape) for _, shape in boxes(cap, f)],
        compiler_params=pltpu.CompilerParams(
            collective_id=1, has_side_effects=True, vmem_limit_bytes=60 * 2**20),
        name="moe_layer",
    )(ids, nums, tokens, grad_out, gate_weight.reshape(split), up_weight.reshape(split), down_weight)

    parts = 4
    return tuple(pl.pallas_call(
        functools.partial(finish, cap, parts),
        out_shape=(like(count, f), like(count, f), like(d, h), like(d, h), like(h, d)),
        in_specs=[vm, vm, vm, anywhere, anywhere, anywhere],
        out_specs=(vm, vm, anywhere, anywhere, anywhere),
        scratch_shapes=[v(2, d, h), v(h, d), pltpu.SemaphoreType.DMA((3, parts)), pltpu.SemaphoreType.DMA((3, parts))],
        compiler_params=pltpu.CompilerParams(vmem_limit_bytes=60 * 2**20),
        name="finish",
    )(ids, nums, home, gg.reshape(d, h), gu.reshape(d, h), gd))


def solution(mesh):
    placed = (
        P("grp", "col"),
        P("grp", "col"),
        P("grp", None),
        P("grp"),
        P(None, ("grp", "col")),
        P(None, ("grp", "col")),
        P(("grp", "col"), None),
    )
    return jax.shard_map(
        body,
        mesh=mesh,
        in_specs=placed,
        out_specs=(
            P("grp", "col"),
            P("grp", "col"),
            P(None, ("grp", "col")),
            P(None, ("grp", "col")),
            P(("grp", "col"), None),
        ),
        check_vma=False,
    )
```

```python
import functools

import jax
import jax.numpy as jnp
from jax import lax
from jax.experimental import pallas as pl
from jax.experimental.pallas import tpu as pltpu
from jax.sharding import PartitionSpec as P

MESH = pl.DeviceIdType.MESH
BF = jnp.bfloat16
F32 = jnp.float32
CHUNKS = 4
ROWS_TOP = (((0,), (0,)), ((), ()))
ROWS_BOTH = (((1,), (1,)), ((), ()))
GATHER = (("Myzx", "Mzyx", "Myzx", "Myzx"), ("Xyz", "Mzxy", "Xzy", "xyz"))
REDUCE = (("xzy", "Xzy", "Xzy", "Xyz"), ("Mzyx", "Mzyx", "MyXz", "Myzx"))
ORDER = (
    "d21", "d01", "g011", "d31", "d00", "d20", "d11", "d10", "d30", "g211", "g012", "g311", "g001", "g111",
    "g201", "g312", "g212", "g101", "g002", "g313", "g202", "g013", "g213", "g112", "g003", "g203", "g301", "g113",
    "g102", "p0", "t0", "s0", "g302", "g314", "t2", "p2", "s2", "v0", "o0", "r001", "b0", "g103",
    "r011", "v2", "b2", "r211", "g303", "p1", "o2", "t1", "s1", "r012", "r201", "p3", "t3", "s3",
    "v1", "r002", "o1", "r101", "r212", "v3", "o3", "r301", "b3", "r311", "b1", "r111", "r202", "n1",
    "r312", "n2", "w0", "r112", "r302", "w1", "r102", "r003", "r013", "n3", "r313", "r203", "w2", "r113",
    "r303", "r103", "r004", "h21", "h01", "h20", "h31", "w3", "h11", "h30", "n0", "h10", "h00",
)


def gather_steps(path):
    axes, steps = path.strip("M"), []
    for i, axis in enumerate(axes):
        if i or path[0] != "M":
            steps += [(axis, axes[:i].lower(), later) for later in range(2 if axis == "x" else 1)]
    return steps


def reduce_steps(path):
    steps = gather_steps(path)
    return sorted(steps, key=lambda step: (-len(step[1]), step[2]))


def boxes(cap, f):
    found = []
    for k in range(CHUNKS):
        for a in range(2):
            for i, (axis, axes, later) in enumerate(reduce_steps(REDUCE[a][k])):
                n = 2 * cap if "z" in axes else cap
                width = f * (4 if "x" in axes else 1) * (2 if "y" in axes else 1)
                top = -(-n // 32) * 16
                rows = [n] * 3 if axis == "X" else [n] if axis != "x" else [n, n] if later else [top, n - top]
                found += [((k, a, i + 1), (some, width)) for some in rows]
    return found


def box_keys():
    return [key for key, _ in boxes(16, 128)]


def place():
    grp, col = lax.axis_index("grp"), lax.axis_index("col")
    return grp // 4, grp % 4, col // 8, (col // 2) % 4, col % 2


def sources(yl, z):
    return [dict(yl=1 - yl if k // 2 else yl, z=3 - z if k % 2 else z) for k in range(CHUNKS)]


def routing(cap, ids, nums, yl, z):
    first, second = ids[0:1, :], ids[1:2, :]
    share = nums[...].astype(F32) / 64.0
    count = first.shape[1]
    has, weight = [], []
    for where in sources(yl, z):
        expert = where["yl"] * 2 + where["z"] // 2
        one, two = first == expert, second == expert
        has.append(jnp.logical_or(one, two).astype(F32))
        weight.append(jnp.where(one, share, 1.0 - share))
    marks = jnp.concatenate(has + [jnp.zeros((4, count), F32)], axis=0)
    before = (lax.broadcasted_iota(jnp.int32, (count, count), 0)
              < lax.broadcasted_iota(jnp.int32, (count, count), 1)).astype(F32)
    position = jnp.dot(marks.astype(BF), before.astype(BF), preferred_element_type=F32)
    slot = lax.broadcasted_iota(jnp.int32, (cap, count), 0).astype(F32)
    found = []
    for k in range(CHUNKS):
        chosen = jnp.where(slot == position[k:k + 1, :], has[k], 0.0)
        found.append((chosen.astype(BF), (chosen * weight[k]).astype(BF)))
    return found


def finish(cap, parts, ids, nums, home, gg, gu, gd, lo, gt, ggo, guo, gdo, done):
    copies = []
    for q, (src, dst) in enumerate(((gg, ggo), (gu, guo), (gd, gdo))):
        rows = src.shape[0] // parts
        for i in range(parts):
            at = pl.ds(i * rows, rows)
            copies.append(pltpu.make_async_copy(src.at[at], dst.at[at], done.at[q, i]))
    for copy in copies:
        copy.start()
    yl, z, _, _, _ = place()
    picks = routing(cap, ids, nums, yl, z)
    for a, out in ((0, lo), (1, gt)):
        total = jnp.zeros(out.shape, F32)
        for k in range(CHUNKS):
            for part in range(2 if REDUCE[a][k][0] == "M" else 1):
                total = total + lax.dot_general(
                    picks[k][1 - a], home[a, k, part], ROWS_TOP, preferred_element_type=F32)
        out[...] = total.astype(BF)
    for copy in copies:
        copy.wait()


def kernel(cap, f, h,
           ids, nums, tok, gout, wg, wu, wd,
           home, gg, gu, gd,
           sent, tbuf, gbuf, wgu, wdn, act_mine, act_theirs, hid, gact, pout, pback,
           gwt, gdt, ss, rs, ls, *landings):
    d2 = 8 * f
    yl, z, yh, x, c = place()
    zl = z % 2
    xr, xl, xo = (x + 1) % 4, (x + 3) % 4, (x + 2) % 4

    def dev(yl=yl, z=z, yh=yh, x=x, c=c):
        return (yl * 4 + z, (yh * 4 + x) * 2 + c)

    right, left = dev(x=xr), dev(x=xl)
    other_y, other_z, other_c = dev(yh=1 - yh), dev(z=z + 1 - 2 * zl), dev(c=1 - c)

    homes = sources(yl, z)

    def beside(k, axis):
        if axis == "y":
            return dev(**homes[k], yh=1 - yh)
        there = homes[k]["z"]
        return dev(yl=homes[k]["yl"], z=there + 1 - 2 * (there % 2))

    counter = [0]
    started = []
    inbox, landing = {}, {}
    for key, box in zip(box_keys(), landings):
        inbox.setdefault(key, []).append(box)

    def send(src, dst, target):
        i = counter[0]
        counter[0] += 1
        copy = pltpu.make_async_remote_copy(
            src_ref=src, dst_ref=dst, send_sem=ss.at[i], recv_sem=rs.at[i],
            device_id=target, device_id_type=MESH)
        copy.start()
        started.append(copy)
        return copy

    def got(copies):
        for copy in copies:
            copy.wait_recv()

    def lanes(off, n):
        return pl.ds(pl.multiple_of(off, 128), n)

    def rws(off, n):
        return pl.ds(pl.multiple_of(off, 16), n)

    def off_a(x, yh):
        return (x * 2 + yh) * f

    def off_b(yh, x):
        return (yh * 4 + x) * f

    def add_into(dst, row, n, off, width, *srcs):
        @pl.loop(0, n // 16)
        def _(i):
            at = (rws(row + i * 16, 16), lanes(off, width))
            total = dst[at].astype(F32)
            for src in srcs:
                total = total + src[rws(i * 16, 16), :].astype(F32)
            dst[at] = total.astype(BF)

    barrier = pltpu.get_barrier_semaphore()
    across = dev(x=xo)
    partners = [right, left, across, other_y, other_z, other_c]
    partners += [dev(**homes[k]) for k in (1, 2, 3)]
    partners += [beside(k, axis) for axis, ks in (("y", (1, 2, 3)), ("z", (1,))) for k in ks]
    for partner in partners:
        pl.semaphore_signal(barrier, inc=1, device_id=partner, device_id_type=MESH)

    for y in range(2):
        for q, w in enumerate((wg, wu)):
            at = (slice(None), y, slice(None), lanes(2 * h * q + h * c, h))
            pltpu.make_async_copy(w.at[y, :, c], wgu.at[at], ls.at[0]).start()
    for p in range(8):
        at = (rws(h * c, h), pl.ds(p * f, f))
        pltpu.make_async_copy(wd.at[:, lanes((p * 2 + c) * f, f)], wdn.at[at], ls.at[3]).start()

    def weights_from_other():
        for y in range(2):
            for q, w in enumerate((wg, wu)):
                at = (slice(None), y, slice(None), lanes(2 * h * q + h * c, h))
                pltpu.make_async_remote_copy(
                    src_ref=w.at[y, :, 1 - c], dst_ref=wgu.at[at], send_sem=ls.at[1], recv_sem=ls.at[2],
                    device_id=other_c, device_id_type=MESH).start()
        for p in range(8):
            at = (rws(h * c, h), pl.ds(p * f, f))
            pltpu.make_async_remote_copy(
                src_ref=wd.at[:, lanes((p * 2 + 1 - c) * f, f)], dst_ref=wdn.at[at], send_sem=ls.at[4],
                recv_sem=ls.at[5], device_id=other_c, device_id_type=MESH).start()

    ready = []

    def weights_ready():
        half_gu = wgu.at[:, :, :, pl.ds(0, 2 * h)]
        half_d = wdn.at[pl.ds(0, h)]
        for i, part in ((0, half_gu), (1, half_gu), (2, half_gu), (3, half_d), (4, half_d), (5, half_d)):
            pltpu.make_async_copy(part, part, ls.at[i]).wait()

    picks = routing(cap, ids, nums, yl, z)
    pend, local = {}, {}
    two = 2 * cap
    bufs = (tbuf, gbuf)
    sums = (pout, pback)

    def region(tokens_first, k, axes, z=zl, x=x, y=yh):
        row, n = (k * two, two) if "z" in axes else (k * two + z * cap, cap)
        if "x" in axes and "y" in axes:
            off, width = 0, d2
        elif tokens_first:
            off, width = (off_a(x, 0), 2 * f) if "y" in axes else (off_a(x, y), f)
        else:
            off, width = (off_b(y, 0), 4 * f) if "x" in axes else (off_b(y, x), f)
        return row, n, off, width

    def view(buf, part):
        row, n, off, width = part
        return buf.at[rws(row, n), lanes(off, width)]

    def halves(part):
        row, n, off, width = part
        top = -(-n // 32) * 16
        return (row, top, off, width), (row + top, n - top, off, width)

    def dispatch(k, a):
        off = (off_a(x, yh), off_b(yh, x))[a]
        theirs = 1 - zl if k % 2 else zl
        sent[a, k] = jnp.dot(picks[k][a], (tok, gout)[a][...], preferred_element_type=F32).astype(BF)
        dst = bufs[a].at[rws(k * two + theirs * cap, cap), lanes(off, f)]
        if k == 0:
            copy = pltpu.make_async_copy(sent.at[a, 0], dst, ls.at[6 + a])
            copy.start()
            local["d", a] = copy
            pend["g", k, a] = []
        else:
            pend["g", k, a] = [send(sent.at[a, k], dst, dev(**homes[k]))]
        path = GATHER[a][k]
        if path[0] == "M":
            pend["g", k, a].append(send(sent.at[a, k], dst, beside(k, path[1])))

    def gathered(k, a):
        if k == 0 and ("d", a) in local:
            local.pop(("d", a)).wait()
        got(pend["g", k, a])

    def gather(k, a, phase):
        gathered(k, a)
        axis, axes, later = gather_steps(GATHER[a][k])[phase - 1]
        buf = bufs[a]
        if axis == "x" and later:
            up = view(buf, halves(region(a == 0, k, axes, x=xl))[0])
            down = view(buf, halves(region(a == 0, k, axes, x=xr))[1])
            pend["g", k, a] = [send(up, up, right), send(down, down, left)]
        else:
            mine = view(buf, region(a == 0, k, axes))
            to = dict(x=(right, left), X=(right, left, across), y=(other_y,), z=(other_z,))[axis]
            pend["g", k, a] = [send(mine, mine, target) for target in to]

    def project_tokens(k):
        gathered(k, 0)
        rows = pl.ds(k * two, two)
        if not ready:
            weights_ready()
            ready.append(True)

        @pl.loop(0, 2)
        def _(n):
            w = wgu[:, :, :, lanes(n * 2 * h, 2 * h)].reshape(d2, 2 * h)
            act_mine[rows, lanes(n * 2 * h, 2 * h)] = jnp.dot(tbuf[rows, :], w, preferred_element_type=F32)

    def project_grads(k):
        gathered(k, 1)
        rows = pl.ds(k * two, two)
        if not ready:
            weights_ready()
            ready.append(True)

        @pl.loop(0, 2)
        def _(n):
            act_mine[rows, lanes((4 + n) * h, h)] = lax.dot_general(
                gbuf[rows, :], wdn[rws(n * h, h), :], ROWS_BOTH, preferred_element_type=F32)

    def swap(k):
        rows = pl.ds(k * two, two)
        pend["p", k] = [send(act_mine.at[rows], act_theirs.at[rows], other_c)]

    def activate(k):
        got(pend["p", k])

        @pl.loop(0, two // 16)
        def _(i):
            rows = rws(k * two + i * 16, 16)
            for n in range(2):
                def both(q):
                    at = (rows, pl.ds((q * 2 + n) * h, h))
                    return act_mine[at] + act_theirs[at]
                gate, up, grad = both(0), both(1), both(2)
                sig = jax.nn.sigmoid(gate)
                silu = gate * sig
                hid[rows, pl.ds(n * h, h)] = (silu * up).astype(BF)
                gact[rows, pl.ds(n * h, h)] = (grad * up * sig * (1.0 + gate * (1.0 - sig))).astype(BF)
                gact[rows, pl.ds((2 + n) * h, h)] = (grad * silu).astype(BF)

    def expand_out(k):
        rows = pl.ds(k * two, two)

        @pl.loop(0, 4)
        def _(n):
            at = lanes(n * 2 * f, 2 * f)
            pout[rows, at] = jnp.dot(hid[rows, :], wdn[:, at], preferred_element_type=F32).astype(BF)

    def expand_back(k):
        rows = pl.ds(k * two, two)

        @pl.loop(0, 4)
        def _(n):
            w = wgu[n].reshape(2 * f, 4 * h)
            pback[rows, lanes(n * 2 * f, 2 * f)] = lax.dot_general(
                gact[rows, :], w, ROWS_BOTH, preferred_element_type=F32).astype(BF)

    def swap_in(k, a, landed):
        got(pend["r", k, a])
        for part, slots in landed:
            row, n, off, width = part
            add_into(sums[a], row, n, off, width, *slots)

    def reduce(k, a, phase):
        if phase > 1:
            swap_in(k, a, landing[k, a])
        axis, axes, later = reduce_steps(REDUCE[a][k])[phase - 1]
        spot = functools.partial(region, a == 1, k, axes)
        slots = inbox[k, a, phase]
        if axis == "X":
            moves = [(spot(x=xr), right), (spot(x=xl), left), (spot(x=xo), across)]
            added = [(spot(), (0, 1, 2))]
        elif axis == "x" and later:
            moves, added = [(spot(x=xr), right), (spot(x=xl), left)], [(spot(), (0, 1))]
        elif axis == "x":
            moves = [(halves(spot(x=xo))[0], right), (halves(spot(x=xo))[1], left)]
            added = [(halves(spot(x=xr))[0], (0,)), (halves(spot(x=xl))[1], (1,))]
        elif axis == "y":
            moves, added = [(spot(y=1 - yh), other_y)], [(spot(), (0,))]
        else:
            moves, added = [(spot(z=1 - zl), other_z)], [(spot(), (0,))]
        pend["r", k, a] = [send(view(sums[a], part), slot, target) for (part, target), slot in zip(moves, slots)]
        landing[k, a] = [(part, [slots[j] for j in which]) for part, which in added]

    def return_home(k, a):
        swap_in(k, a, landing[k, a])
        spot = functools.partial(region, a == 1, k, "")
        mine, path = view(sums[a], spot()), REDUCE[a][k]
        pend["h", k, a] = []
        if k == 0:
            local["h", a] = pltpu.make_async_copy(mine, home.at[a, 0, 0], ls.at[8 + a])
            local["h", a].start()
        else:
            pend["h", k, a].append(send(mine, home.at[a, k, 0], dev(**homes[k])))
        if path[0] == "M":
            theirs = view(sums[a], spot(y=1 - yh) if path[1] == "y" else spot(z=1 - zl))
            pend["h", k, a].append(send(theirs, home.at[a, k, 1], beside(k, path[1])))

    def weight_grads_up(part):
        @pl.loop(part * 2, part * 2 + 2)
        def _(p):
            there = rws((((p % 2) * 4 + p // 2) * 2 + c) * f, f)
            for q, out in enumerate((gg, gu)):
                def product(core):
                    return lax.dot_general(
                        tbuf[:, lanes(p * f, f)], gact[:, lanes(2 * h * q + h * core, h)], ROWS_TOP,
                        preferred_element_type=F32).astype(BF)
                gwt[q, p] = product(1 - c)
                pltpu.make_async_remote_copy(
                    src_ref=gwt.at[q, p], dst_ref=out.at[there], send_sem=ls.at[11], recv_sem=ls.at[12],
                    device_id=other_c, device_id_type=MESH).start()
                out[there, :] = product(c)

    def weight_grads_down(part):
        @pl.loop(part * 2, part * 2 + 2)
        def _(p):
            there = lanes((p * 2 + c) * f, f)
            def product(core):
                return lax.dot_general(
                    hid[:, lanes(h * core, h)], gbuf[:, lanes(p * f, f)], ROWS_TOP,
                    preferred_element_type=F32).astype(BF)
            gdt[p] = product(1 - c)
            pltpu.make_async_remote_copy(
                src_ref=gdt.at[p], dst_ref=gd.at[:, there], send_sem=ls.at[14], recv_sem=ls.at[15],
                device_id=other_c, device_id_type=MESH).start()
            gd[:, there] = product(c)

    def weight_grads_done():
        for i, part in ((11, gwt), (12, gwt), (14, gdt), (15, gdt)):
            pltpu.make_async_copy(part, part, ls.at[i]).wait()

    steps = dict(d=dispatch, g=gather, t=project_tokens, p=project_grads, s=swap, v=activate, o=expand_out,
                 b=expand_back, r=reduce, h=return_home, w=weight_grads_up, n=weight_grads_down)
    pl.semaphore_wait(barrier, len(partners))
    drained = 0
    for i, step in enumerate(ORDER):
        steps[step[0]](*(int(digit) for digit in step[1:]))
        if i == 11:
            weights_from_other()
        old = max(len(started) - 40, 0)
        for copy in started[drained:old]:
            copy.wait_send()
        drained = old
    weight_grads_done()
    for copy in started[drained:]:
        copy.wait_send()
    for a in range(2):
        local["h", a].wait()
        for k in range(CHUNKS):
            got(pend["h", k, a])


def body(tokens, grad_out, expert_ids, gate_num, gate_weight, up_weight, down_weight):
    count, f = tokens.shape
    d, h = gate_weight.shape
    cap = 5 * count // 8
    rows, d2 = 8 * cap, 8 * f
    ids, nums = expert_ids.T, gate_num.reshape(1, count)
    split = (2, 4, 2, f, h)
    vm = pl.BlockSpec(memory_space=pltpu.VMEM)
    anywhere = pl.BlockSpec(memory_space=pl.ANY)

    def v(*shape, dtype=BF):
        return pltpu.VMEM(shape, dtype)

    def like(*shape):
        return jax.ShapeDtypeStruct(shape, BF)

    sems = 128
    home, gg, gu, gd = pl.pallas_call(
        functools.partial(kernel, cap, f, h),
        out_shape=(v(2, CHUNKS, 2, cap, f), v(d, h), v(d, h), v(h, d)),
        in_specs=[vm, vm, vm, vm, anywhere, anywhere, anywhere],
        out_specs=(vm, vm, vm, vm),
        scratch_shapes=[
            v(2, CHUNKS, cap, f), v(rows, d2), v(rows, d2),
            v(4, 2, f, 4 * h), v(2 * h, d2),
            v(rows, 6 * h, dtype=F32), v(rows, 6 * h, dtype=F32), v(rows, 2 * h), v(rows, 4 * h),
            v(rows, d2), v(rows, d2),
            v(2, 8, f, h), v(8, h, f),
            pltpu.SemaphoreType.DMA((sems,)), pltpu.SemaphoreType.DMA((sems,)), pltpu.SemaphoreType.DMA((16,)),
        ] + [v(*shape) for _, shape in boxes(cap, f)],
        compiler_params=pltpu.CompilerParams(
            collective_id=1, has_side_effects=True, vmem_limit_bytes=49 * 2**20),
        name="moe_layer",
    )(ids, nums, tokens, grad_out, gate_weight.reshape(split), up_weight.reshape(split), down_weight)

    parts = 4
    return tuple(pl.pallas_call(
        functools.partial(finish, cap, parts),
        out_shape=(like(count, f), like(count, f), like(d, h), like(d, h), like(h, d)),
        in_specs=[vm, vm, vm, vm, vm, vm],
        out_specs=(vm, vm, anywhere, anywhere, anywhere),
        scratch_shapes=[pltpu.SemaphoreType.DMA((3, parts))],
        compiler_params=pltpu.CompilerParams(vmem_limit_bytes=16 * 2**20),
        name="finish",
    )(ids, nums, home, gg, gu, gd))


def solution(mesh):
    placed = (
        P("grp", "col"),
        P("grp", "col"),
        P("grp", None),
        P("grp"),
        P(None, ("grp", "col")),
        P(None, ("grp", "col")),
        P(("grp", "col"), None),
    )
    return jax.shard_map(
        body,
        mesh=mesh,
        in_specs=placed,
        out_specs=(
            P("grp", "col"),
            P("grp", "col"),
            P(None, ("grp", "col")),
            P(None, ("grp", "col")),
            P(("grp", "col"), None),
        ),
        check_vma=False,
    )
```

```python
import functools

import jax
import jax.numpy as jnp
from jax import lax
from jax.experimental import pallas as pl
from jax.experimental.pallas import tpu as pltpu
from jax.sharding import PartitionSpec as P

MESH = pl.DeviceIdType.MESH
BF = jnp.bfloat16
F32 = jnp.float32
CHUNKS = 4
ROWS_TOP = (((0,), (0,)), ((), ()))
ROWS_BOTH = (((1,), (1,)), ((), ()))
GATHER = (("yzx", "zyx", "zyx", "yzx"), ("Xyz", "Xzy", "xyz", "zxy"))
REDUCE = (("xyz", "Xyz", "Xzy", "Xyz"), ("Mzyx", "Mzyx", "Myzx", "Myzx"))
ORDER = (
    "d00", "d01", "g001", "d11", "g011", "d21", "d31", "d20", "d10", "g002", "g111", "g101", "g012", "g211",
    "g311", "g201", "g003", "d30", "g112", "g102", "g212", "g312", "g013", "g202", "g301", "g004", "g103", "g213",
    "g203", "g113", "t0", "g313", "g302", "g214", "p0", "s0", "g104", "g204", "g303", "v0", "o0", "b0",
    "g314", "r001", "t1", "p1", "s1", "r011", "t2", "p2", "s2", "v1", "g304", "b1", "r111", "v2",
    "o2", "r201", "r012", "o1", "r101", "t3", "r002", "p3", "s3", "r112", "b2", "v3", "o3", "r301",
    "r211", "b3", "r311", "r102", "n0", "r212", "w0", "r202", "r113", "r312", "r003", "w3", "r302", "n3",
    "r013", "r103", "r213", "n1", "n2", "r203", "r313", "w1", "r303", "h21", "h10", "h11", "r004", "h31",
    "h20", "w2", "h01", "h30", "h00",
)


def gather_steps(path):
    axes, steps = path.strip("M"), []
    for i, axis in enumerate(axes):
        if i or path[0] != "M":
            steps += [(axis, axes[:i].lower(), later) for later in range(2 if axis == "x" else 1)]
    return steps


def reduce_steps(path):
    steps = gather_steps(path)
    return sorted(steps, key=lambda step: (-len(step[1]), step[2]))


def boxes(cap, f):
    found = []
    for k in range(CHUNKS):
        for a in range(2):
            for i, (axis, axes, later) in enumerate(reduce_steps(REDUCE[a][k])):
                n = 2 * cap if "z" in axes else cap
                width = f * (4 if "x" in axes else 1) * (2 if "y" in axes else 1)
                top = -(-n // 32) * 16
                rows = [n] * 3 if axis == "X" else [n] if axis != "x" else [n, n] if later else [top, n - top]
                found += [((k, a, i + 1), (some, width)) for some in rows]
    return found


def box_keys():
    return [key for key, _ in boxes(16, 128)]


def place():
    grp, col = lax.axis_index("grp"), lax.axis_index("col")
    return grp // 4, grp % 4, col // 8, (col // 2) % 4, col % 2


def sources(yl, z):
    return [dict(yl=1 - yl if k // 2 else yl, z=3 - z if k % 2 else z) for k in range(CHUNKS)]


def routing(cap, ids, nums, yl, z):
    first, second = ids[0:1, :], ids[1:2, :]
    share = nums[...].astype(F32) / 64.0
    count = first.shape[1]
    has, weight = [], []
    for where in sources(yl, z):
        expert = where["yl"] * 2 + where["z"] // 2
        one, two = first == expert, second == expert
        has.append(jnp.logical_or(one, two).astype(F32))
        weight.append(jnp.where(one, share, 1.0 - share))
    marks = jnp.concatenate(has + [jnp.zeros((4, count), F32)], axis=0)
    before = (lax.broadcasted_iota(jnp.int32, (count, count), 0)
              < lax.broadcasted_iota(jnp.int32, (count, count), 1)).astype(F32)
    position = jnp.dot(marks.astype(BF), before.astype(BF), preferred_element_type=F32)
    slot = lax.broadcasted_iota(jnp.int32, (cap, count), 0).astype(F32)
    found = []
    for k in range(CHUNKS):
        chosen = jnp.where(slot == position[k:k + 1, :], has[k], 0.0)
        found.append((chosen.astype(BF), (chosen * weight[k]).astype(BF)))
    return found


def finish(cap, parts, ids, nums, home, gg, gu, gd, lo, gt, ggo, guo, gdo, done):
    copies = []
    for q, (src, dst) in enumerate(((gg, ggo), (gu, guo), (gd, gdo))):
        rows = src.shape[0] // parts
        for i in range(parts):
            at = pl.ds(i * rows, rows)
            copies.append(pltpu.make_async_copy(src.at[at], dst.at[at], done.at[q, i]))
    for copy in copies:
        copy.start()
    yl, z, _, _, _ = place()
    picks = routing(cap, ids, nums, yl, z)
    for a, out in ((0, lo), (1, gt)):
        total = jnp.zeros(out.shape, F32)
        for k in range(CHUNKS):
            for part in range(2 if REDUCE[a][k][0] == "M" else 1):
                total = total + lax.dot_general(
                    picks[k][1 - a], home[a, k, part], ROWS_TOP, preferred_element_type=F32)
        out[...] = total.astype(BF)
    for copy in copies:
        copy.wait()


def kernel(cap, f, h,
           ids, nums, tok, gout, wg, wu, wd,
           home, gg, gu, gd,
           tok_in, gout_in, sent, tbuf, gbuf, wgu, wdn, act_mine, act_theirs, hid, gact, pout, pback,
           gwt, gdt, ss, rs, ls, *landings):
    d2 = 8 * f
    yl, z, yh, x, c = place()
    zl = z % 2
    xr, xl, xo = (x + 1) % 4, (x + 3) % 4, (x + 2) % 4

    def dev(yl=yl, z=z, yh=yh, x=x, c=c):
        return (yl * 4 + z, (yh * 4 + x) * 2 + c)

    right, left = dev(x=xr), dev(x=xl)
    other_y, other_z, other_c = dev(yh=1 - yh), dev(z=z + 1 - 2 * zl), dev(c=1 - c)

    homes = sources(yl, z)

    def beside(k, axis):
        if axis == "y":
            return dev(**homes[k], yh=1 - yh)
        there = homes[k]["z"]
        return dev(yl=homes[k]["yl"], z=there + 1 - 2 * (there % 2))

    counter = [0]
    started = []
    inbox, landing = {}, {}
    for key, box in zip(box_keys(), landings):
        inbox.setdefault(key, []).append(box)

    def send(src, dst, target):
        i = counter[0]
        counter[0] += 1
        copy = pltpu.make_async_remote_copy(
            src_ref=src, dst_ref=dst, send_sem=ss.at[i], recv_sem=rs.at[i],
            device_id=target, device_id_type=MESH)
        copy.start()
        started.append(copy)
        return copy

    def got(copies):
        for copy in copies:
            copy.wait_recv()

    def lanes(off, n):
        return pl.ds(pl.multiple_of(off, 128), n)

    def rws(off, n):
        return pl.ds(pl.multiple_of(off, 16), n)

    def off_a(x, yh):
        return (x * 2 + yh) * f

    def off_b(yh, x):
        return (yh * 4 + x) * f

    def add_into(dst, row, n, off, width, *srcs):
        @pl.loop(0, n // 16)
        def _(i):
            at = (rws(row + i * 16, 16), lanes(off, width))
            total = dst[at].astype(F32)
            for src in srcs:
                total = total + src[rws(i * 16, 16), :].astype(F32)
            dst[at] = total.astype(BF)

    barrier = pltpu.get_barrier_semaphore()
    across = dev(x=xo)
    partners = [right, left, across, other_y, other_z, other_c]
    partners += [dev(**homes[k]) for k in (1, 2, 3)]
    partners += [beside(k, axis) for axis, ks in (("y", (1, 2, 3)), ("z", (1,))) for k in ks]
    for partner in partners:
        pl.semaphore_signal(barrier, inc=1, device_id=partner, device_id_type=MESH)

    taken = [pltpu.make_async_copy(src, dst, ls.at[10 + 3 * i])
             for i, (src, dst) in enumerate(((tok, tok_in), (gout, gout_in)))]
    for copy in taken:
        copy.start()

    for y in range(2):
        for q, w in enumerate((wg, wu)):
            at = (slice(None), y, slice(None), lanes(2 * h * q + h * c, h))
            pltpu.make_async_copy(w.at[y, :, c], wgu.at[at], ls.at[0]).start()
    for p in range(8):
        at = (rws(h * c, h), pl.ds(p * f, f))
        pltpu.make_async_copy(wd.at[:, lanes((p * 2 + c) * f, f)], wdn.at[at], ls.at[3]).start()

    def weights_from_other():
        for y in range(2):
            for q, w in enumerate((wg, wu)):
                at = (slice(None), y, slice(None), lanes(2 * h * q + h * c, h))
                pltpu.make_async_remote_copy(
                    src_ref=w.at[y, :, 1 - c], dst_ref=wgu.at[at], send_sem=ls.at[1], recv_sem=ls.at[2],
                    device_id=other_c, device_id_type=MESH).start()
        for p in range(8):
            at = (rws(h * c, h), pl.ds(p * f, f))
            pltpu.make_async_remote_copy(
                src_ref=wd.at[:, lanes((p * 2 + 1 - c) * f, f)], dst_ref=wdn.at[at], send_sem=ls.at[4],
                recv_sem=ls.at[5], device_id=other_c, device_id_type=MESH).start()

    ready = []

    def weights_ready():
        half_gu = wgu.at[:, :, :, pl.ds(0, 2 * h)]
        half_d = wdn.at[pl.ds(0, h)]
        for i, part in ((0, half_gu), (1, half_gu), (2, half_gu), (3, half_d), (4, half_d), (5, half_d)):
            pltpu.make_async_copy(part, part, ls.at[i]).wait()

    picks = routing(cap, ids, nums, yl, z)
    for copy in taken:
        copy.wait()
    pend, local = {}, {}
    two = 2 * cap
    bufs = (tbuf, gbuf)
    sums = (pout, pback)

    def region(tokens_first, k, axes, z=zl, x=x, y=yh):
        row, n = (k * two, two) if "z" in axes else (k * two + z * cap, cap)
        if "x" in axes and "y" in axes:
            off, width = 0, d2
        elif tokens_first:
            off, width = (off_a(x, 0), 2 * f) if "y" in axes else (off_a(x, y), f)
        else:
            off, width = (off_b(y, 0), 4 * f) if "x" in axes else (off_b(y, x), f)
        return row, n, off, width

    def view(buf, part):
        row, n, off, width = part
        return buf.at[rws(row, n), lanes(off, width)]

    def halves(part):
        row, n, off, width = part
        top = -(-n // 32) * 16
        return (row, top, off, width), (row + top, n - top, off, width)

    def dispatch(k, a):
        off = (off_a(x, yh), off_b(yh, x))[a]
        theirs = 1 - zl if k % 2 else zl
        sent[a, k] = jnp.dot(picks[k][a], (tok_in, gout_in)[a][...], preferred_element_type=F32).astype(BF)
        dst = bufs[a].at[rws(k * two + theirs * cap, cap), lanes(off, f)]
        if k == 0:
            copy = pltpu.make_async_copy(sent.at[a, 0], dst, ls.at[6 + a])
            copy.start()
            local["d", a] = copy
            pend["g", k, a] = []
        else:
            pend["g", k, a] = [send(sent.at[a, k], dst, dev(**homes[k]))]
        path = GATHER[a][k]
        if path[0] == "M":
            pend["g", k, a].append(send(sent.at[a, k], dst, beside(k, path[1])))

    def gathered(k, a):
        if k == 0 and ("d", a) in local:
            local.pop(("d", a)).wait()
        got(pend["g", k, a])

    def gather(k, a, phase):
        gathered(k, a)
        axis, axes, later = gather_steps(GATHER[a][k])[phase - 1]
        buf = bufs[a]
        if axis == "x" and later:
            up = view(buf, halves(region(a == 0, k, axes, x=xl))[0])
            down = view(buf, halves(region(a == 0, k, axes, x=xr))[1])
            pend["g", k, a] = [send(up, up, right), send(down, down, left)]
        else:
            mine = view(buf, region(a == 0, k, axes))
            to = dict(x=(right, left), X=(right, left, across), y=(other_y,), z=(other_z,))[axis]
            pend["g", k, a] = [send(mine, mine, target) for target in to]

    def project_tokens(k):
        gathered(k, 0)
        rows = pl.ds(k * two, two)
        if not ready:
            weights_ready()
            ready.append(True)

        @pl.loop(0, 2)
        def _(n):
            w = wgu[:, :, :, lanes(n * 2 * h, 2 * h)].reshape(d2, 2 * h)
            act_mine[rows, lanes(n * 2 * h, 2 * h)] = jnp.dot(tbuf[rows, :], w, preferred_element_type=F32)

    def project_grads(k):
        gathered(k, 1)
        rows = pl.ds(k * two, two)
        if not ready:
            weights_ready()
            ready.append(True)

        @pl.loop(0, 2)
        def _(n):
            act_mine[rows, lanes((4 + n) * h, h)] = lax.dot_general(
                gbuf[rows, :], wdn[rws(n * h, h), :], ROWS_BOTH, preferred_element_type=F32)

    def swap(k):
        rows = pl.ds(k * two, two)
        pend["p", k] = [send(act_mine.at[rows], act_theirs.at[rows], other_c)]

    def activate(k):
        got(pend["p", k])

        @pl.loop(0, two // 16)
        def _(i):
            rows = rws(k * two + i * 16, 16)
            for n in range(2):
                def both(q):
                    at = (rows, pl.ds((q * 2 + n) * h, h))
                    return act_mine[at] + act_theirs[at]
                gate, up, grad = both(0), both(1), both(2)
                sig = jax.nn.sigmoid(gate)
                silu = gate * sig
                hid[rows, pl.ds(n * h, h)] = (silu * up).astype(BF)
                gact[rows, pl.ds(n * h, h)] = (grad * up * sig * (1.0 + gate * (1.0 - sig))).astype(BF)
                gact[rows, pl.ds((2 + n) * h, h)] = (grad * silu).astype(BF)

    def expand_out(k):
        rows = pl.ds(k * two, two)

        @pl.loop(0, 4)
        def _(n):
            at = lanes(n * 2 * f, 2 * f)
            pout[rows, at] = jnp.dot(hid[rows, :], wdn[:, at], preferred_element_type=F32).astype(BF)

    def expand_back(k):
        rows = pl.ds(k * two, two)

        @pl.loop(0, 4)
        def _(n):
            w = wgu[n].reshape(2 * f, 4 * h)
            pback[rows, lanes(n * 2 * f, 2 * f)] = lax.dot_general(
                gact[rows, :], w, ROWS_BOTH, preferred_element_type=F32).astype(BF)

    def swap_in(k, a, landed):
        got(pend["r", k, a])
        for part, slots in landed:
            row, n, off, width = part
            add_into(sums[a], row, n, off, width, *slots)

    def reduce(k, a, phase):
        if phase > 1:
            swap_in(k, a, landing[k, a])
        axis, axes, later = reduce_steps(REDUCE[a][k])[phase - 1]
        spot = functools.partial(region, a == 1, k, axes)
        slots = inbox[k, a, phase]
        if axis == "X":
            moves = [(spot(x=xr), right), (spot(x=xl), left), (spot(x=xo), across)]
            added = [(spot(), (0, 1, 2))]
        elif axis == "x" and later:
            moves, added = [(spot(x=xr), right), (spot(x=xl), left)], [(spot(), (0, 1))]
        elif axis == "x":
            moves = [(halves(spot(x=xo))[0], right), (halves(spot(x=xo))[1], left)]
            added = [(halves(spot(x=xr))[0], (0,)), (halves(spot(x=xl))[1], (1,))]
        elif axis == "y":
            moves, added = [(spot(y=1 - yh), other_y)], [(spot(), (0,))]
        else:
            moves, added = [(spot(z=1 - zl), other_z)], [(spot(), (0,))]
        pend["r", k, a] = [send(view(sums[a], part), slot, target) for (part, target), slot in zip(moves, slots)]
        landing[k, a] = [(part, [slots[j] for j in which]) for part, which in added]

    def return_home(k, a):
        swap_in(k, a, landing[k, a])
        spot = functools.partial(region, a == 1, k, "")
        mine, path = view(sums[a], spot()), REDUCE[a][k]
        pend["h", k, a] = []
        if k == 0:
            local["h", a] = pltpu.make_async_copy(mine, home.at[a, 0, 0], ls.at[8 + a])
            local["h", a].start()
        else:
            pend["h", k, a].append(send(mine, home.at[a, k, 0], dev(**homes[k])))
        if path[0] == "M":
            theirs = view(sums[a], spot(y=1 - yh) if path[1] == "y" else spot(z=1 - zl))
            pend["h", k, a].append(send(theirs, home.at[a, k, 1], beside(k, path[1])))

    def weight_grads_up(part):
        @pl.loop(part * 2, part * 2 + 2)
        def _(p):
            there = rws((((p % 2) * 4 + p // 2) * 2 + c) * f, f)
            for q, out in enumerate((gg, gu)):
                def product(core):
                    return lax.dot_general(
                        tbuf[:, lanes(p * f, f)], gact[:, lanes(2 * h * q + h * core, h)], ROWS_TOP,
                        preferred_element_type=F32).astype(BF)
                gwt[q, p] = product(1 - c)
                pltpu.make_async_remote_copy(
                    src_ref=gwt.at[q, p], dst_ref=out.at[there], send_sem=ls.at[11], recv_sem=ls.at[12],
                    device_id=other_c, device_id_type=MESH).start()
                out[there, :] = product(c)

    def weight_grads_down(part):
        @pl.loop(part * 2, part * 2 + 2)
        def _(p):
            there = lanes((p * 2 + c) * f, f)
            def product(core):
                return lax.dot_general(
                    hid[:, lanes(h * core, h)], gbuf[:, lanes(p * f, f)], ROWS_TOP,
                    preferred_element_type=F32).astype(BF)
            gdt[p] = product(1 - c)
            pltpu.make_async_remote_copy(
                src_ref=gdt.at[p], dst_ref=gd.at[:, there], send_sem=ls.at[14], recv_sem=ls.at[15],
                device_id=other_c, device_id_type=MESH).start()
            gd[:, there] = product(c)

    def weight_grads_done():
        for i, part in ((11, gwt), (12, gwt), (14, gdt), (15, gdt)):
            pltpu.make_async_copy(part, part, ls.at[i]).wait()

    steps = dict(d=dispatch, g=gather, t=project_tokens, p=project_grads, s=swap, v=activate, o=expand_out,
                 b=expand_back, r=reduce, h=return_home, w=weight_grads_up, n=weight_grads_down)
    pl.semaphore_wait(barrier, len(partners))
    drained = 0
    for i, step in enumerate(ORDER):
        steps[step[0]](*(int(digit) for digit in step[1:]))
        if i == 11:
            weights_from_other()
        old = max(len(started) - 40, 0)
        for copy in started[drained:old]:
            copy.wait_send()
        drained = old
    weight_grads_done()
    for copy in started[drained:]:
        copy.wait_send()
    for a in range(2):
        local["h", a].wait()
        for k in range(CHUNKS):
            got(pend["h", k, a])


def body(tokens, grad_out, expert_ids, gate_num, gate_weight, up_weight, down_weight):
    count, f = tokens.shape
    d, h = gate_weight.shape
    cap = 5 * count // 8
    rows, d2 = 8 * cap, 8 * f
    ids, nums = expert_ids.T, gate_num.reshape(1, count)
    split = (2, 4, 2, f, h)
    vm = pl.BlockSpec(memory_space=pltpu.VMEM)
    anywhere = pl.BlockSpec(memory_space=pl.ANY)

    def v(*shape, dtype=BF):
        return pltpu.VMEM(shape, dtype)

    def like(*shape):
        return jax.ShapeDtypeStruct(shape, BF)

    sems = 128
    home, gg, gu, gd = pl.pallas_call(
        functools.partial(kernel, cap, f, h),
        out_shape=(v(2, CHUNKS, 2, cap, f), v(d, h), v(d, h), v(h, d)),
        in_specs=[vm, vm, anywhere, anywhere, anywhere, anywhere, anywhere],
        out_specs=(vm, vm, vm, vm),
        scratch_shapes=[
            v(count, f), v(count, f), v(2, CHUNKS, cap, f), v(rows, d2), v(rows, d2),
            v(4, 2, f, 4 * h), v(2 * h, d2),
            v(rows, 6 * h, dtype=F32), v(rows, 6 * h, dtype=F32), v(rows, 2 * h), v(rows, 4 * h),
            v(rows, d2), v(rows, d2),
            v(2, 8, f, h), v(8, h, f),
            pltpu.SemaphoreType.DMA((sems,)), pltpu.SemaphoreType.DMA((sems,)), pltpu.SemaphoreType.DMA((16,)),
        ] + [v(*shape) for _, shape in boxes(cap, f)],
        compiler_params=pltpu.CompilerParams(
            collective_id=1, has_side_effects=True, vmem_limit_bytes=49 * 2**20),
        name="moe_layer",
    )(ids, nums, tokens, grad_out, gate_weight.reshape(split), up_weight.reshape(split), down_weight)

    parts = 4
    return tuple(pl.pallas_call(
        functools.partial(finish, cap, parts),
        out_shape=(like(count, f), like(count, f), like(d, h), like(d, h), like(h, d)),
        in_specs=[vm, vm, vm, vm, vm, vm],
        out_specs=(vm, vm, anywhere, anywhere, anywhere),
        scratch_shapes=[pltpu.SemaphoreType.DMA((3, parts))],
        compiler_params=pltpu.CompilerParams(vmem_limit_bytes=16 * 2**20),
        name="finish",
    )(ids, nums, home, gg, gu, gd))


def solution(mesh):
    placed = (
        P("grp", "col"),
        P("grp", "col"),
        P("grp", None),
        P("grp"),
        P(None, ("grp", "col")),
        P(None, ("grp", "col")),
        P(("grp", "col"), None),
    )
    return jax.shard_map(
        body,
        mesh=mesh,
        in_specs=placed,
        out_specs=(
            P("grp", "col"),
            P("grp", "col"),
            P(None, ("grp", "col")),
            P(None, ("grp", "col")),
            P(("grp", "col"), None),
        ),
        check_vma=False,
    )
```

```python
import functools

import jax
import jax.numpy as jnp
from jax import lax
from jax.experimental import pallas as pl
from jax.experimental.pallas import tpu as pltpu
from jax.sharding import PartitionSpec as P

MESH = pl.DeviceIdType.MESH
BF = jnp.bfloat16
F32 = jnp.float32
CHUNKS = 4
ROWS_TOP = (((0,), (0,)), ((), ()))
ROWS_BOTH = (((1,), (1,)), ((), ()))
GATHER = (("zyx", "yzx", "Myzx", "zyx"), ("Xzy", "xyz", "Xyz", "xzy"))
REDUCE = (("Xzy", "Mzxy", "xyz", "Xyz"), ("Myzx", "Mzyx", "Myzx", "Myzx"))
ORDER = (
    "d21", "d00", "d01", "d31", "g001", "g011", "d11", "d10", "d20", "g002", "g211", "g012", "g311", "g101",
    "g201", "g111", "d30", "g212", "g003", "g013", "g112", "g301", "g312", "g102", "g202", "g213", "g302", "g313",
    "g004", "g113", "g203", "g103", "t0", "p0", "s0", "t2", "g303", "p2", "s2", "v0", "o0", "g314",
    "g114", "g104", "b0", "v2", "r011", "g304", "r001", "b2", "o2", "r211", "r201", "r012", "t1", "p1",
    "s1", "t3", "r212", "p3", "v1", "s3", "o1", "r101", "b1", "r111", "v3", "o3", "r301", "b3",
    "r311", "r202", "r013", "r112", "w3", "r213", "w0", "r102", "r312", "r002", "r302", "w2", "n2", "r203",
    "r103", "r113", "n3", "n0", "r313", "r204", "h21", "h01", "r303", "h10", "r003", "h11", "h31", "h20",
    "w1", "h30", "n1", "h00",
)


def gather_steps(path):
    axes, steps = path.strip("M"), []
    for i, axis in enumerate(axes):
        if i or path[0] != "M":
            steps += [(axis, axes[:i].lower(), later) for later in range(2 if axis == "x" else 1)]
    return steps


def reduce_steps(path):
    steps = gather_steps(path)
    return sorted(steps, key=lambda step: (-len(step[1]), step[2]))


def boxes(cap, f):
    found = []
    for k in range(CHUNKS):
        for a in range(2):
            for i, (axis, axes, later) in enumerate(reduce_steps(REDUCE[a][k])):
                n = 2 * cap if "z" in axes else cap
                width = f * (4 if "x" in axes else 1) * (2 if "y" in axes else 1)
                top = -(-n // 32) * 16
                rows = [n] * 3 if axis == "X" else [n] if axis != "x" else [n, n] if later else [top, n - top]
                found += [((k, a, i + 1), (some, width)) for some in rows]
    return found


def box_keys():
    return [key for key, _ in boxes(16, 128)]


def place():
    grp, col = lax.axis_index("grp"), lax.axis_index("col")
    return grp // 4, grp % 4, col // 8, (col // 2) % 4, col % 2


def sources(yl, z):
    return [dict(yl=1 - yl if k // 2 else yl, z=3 - z if k % 2 else z) for k in range(CHUNKS)]


def routing(cap, ids, nums, yl, z):
    first, second = ids[0:1, :], ids[1:2, :]
    share = nums[...].astype(F32) / 64.0
    count = first.shape[1]
    has, weight = [], []
    for where in sources(yl, z):
        expert = where["yl"] * 2 + where["z"] // 2
        one, two = first == expert, second == expert
        has.append(jnp.logical_or(one, two).astype(F32))
        weight.append(jnp.where(one, share, 1.0 - share))
    marks = jnp.concatenate(has + [jnp.zeros((4, count), F32)], axis=0)
    before = (lax.broadcasted_iota(jnp.int32, (count, count), 0)
              < lax.broadcasted_iota(jnp.int32, (count, count), 1)).astype(F32)
    position = jnp.dot(marks.astype(BF), before.astype(BF), preferred_element_type=F32)
    slot = lax.broadcasted_iota(jnp.int32, (cap, count), 0).astype(F32)
    found = []
    for k in range(CHUNKS):
        chosen = jnp.where(slot == position[k:k + 1, :], has[k], 0.0)
        found.append((chosen.astype(BF), (chosen * weight[k]).astype(BF)))
    return found


def finish(cap, parts, ids, nums, home, gg, gu, gd, lo, gt, ggo, guo, gdo, done):
    copies = []
    for q, (src, dst) in enumerate(((gg, ggo), (gu, guo), (gd, gdo))):
        rows = src.shape[0] // parts
        for i in range(parts):
            at = pl.ds(i * rows, rows)
            copies.append(pltpu.make_async_copy(src.at[at], dst.at[at], done.at[q, i]))
    for copy in copies:
        copy.start()
    yl, z, _, _, _ = place()
    picks = routing(cap, ids, nums, yl, z)
    for a, out in ((0, lo), (1, gt)):
        total = jnp.zeros(out.shape, F32)
        for k in range(CHUNKS):
            for part in range(2 if REDUCE[a][k][0] == "M" else 1):
                total = total + lax.dot_general(
                    picks[k][1 - a], home[a, k, part], ROWS_TOP, preferred_element_type=F32)
        out[...] = total.astype(BF)
    for copy in copies:
        copy.wait()


def kernel(cap, f, h,
           ids, nums, tok, gout, wg, wu, wd,
           home, gg, gu, gd,
           tok_in, gout_in, sent, tbuf, gbuf, wgu, wdn, act_mine, act_theirs, hid, gact, pout, pback,
           gwt, gdt, ss, rs, ls, *landings):
    d2 = 8 * f
    yl, z, yh, x, c = place()
    zl = z % 2
    xr, xl, xo = (x + 1) % 4, (x + 3) % 4, (x + 2) % 4

    def dev(yl=yl, z=z, yh=yh, x=x, c=c):
        return (yl * 4 + z, (yh * 4 + x) * 2 + c)

    right, left = dev(x=xr), dev(x=xl)
    other_y, other_z, other_c = dev(yh=1 - yh), dev(z=z + 1 - 2 * zl), dev(c=1 - c)

    homes = sources(yl, z)

    def beside(k, axis):
        if axis == "y":
            return dev(**homes[k], yh=1 - yh)
        there = homes[k]["z"]
        return dev(yl=homes[k]["yl"], z=there + 1 - 2 * (there % 2))

    counter = [0]
    started = []
    inbox, landing = {}, {}
    for key, box in zip(box_keys(), landings):
        inbox.setdefault(key, []).append(box)

    def send(src, dst, target):
        i = counter[0]
        counter[0] += 1
        copy = pltpu.make_async_remote_copy(
            src_ref=src, dst_ref=dst, send_sem=ss.at[i], recv_sem=rs.at[i],
            device_id=target, device_id_type=MESH)
        copy.start()
        started.append(copy)
        return copy

    def got(copies):
        for copy in copies:
            copy.wait_recv()

    def lanes(off, n):
        return pl.ds(pl.multiple_of(off, 128), n)

    def rws(off, n):
        return pl.ds(pl.multiple_of(off, 16), n)

    def off_a(x, yh):
        return (x * 2 + yh) * f

    def off_b(yh, x):
        return (yh * 4 + x) * f

    def add_into(dst, row, n, off, width, *srcs):
        @pl.loop(0, n // 16)
        def _(i):
            at = (rws(row + i * 16, 16), lanes(off, width))
            total = dst[at].astype(F32)
            for src in srcs:
                total = total + src[rws(i * 16, 16), :].astype(F32)
            dst[at] = total.astype(BF)

    barrier = pltpu.get_barrier_semaphore()
    across = dev(x=xo)
    partners = [right, left, across, other_y, other_z, other_c]
    partners += [dev(**homes[k]) for k in (1, 2, 3)]
    partners += [beside(k, axis) for axis, ks in (("y", (1, 2, 3)), ("z", (1,))) for k in ks]
    for partner in partners:
        pl.semaphore_signal(barrier, inc=1, device_id=partner, device_id_type=MESH)

    taken = [pltpu.make_async_copy(src, dst, ls.at[10 + 3 * i])
             for i, (src, dst) in enumerate(((tok, tok_in), (gout, gout_in)))]
    for copy in taken:
        copy.start()

    for y in range(2):
        for q, w in enumerate((wg, wu)):
            at = (slice(None), y, slice(None), lanes(2 * h * q + h * c, h))
            pltpu.make_async_copy(w.at[y, :, c], wgu.at[at], ls.at[0]).start()
    for p in range(8):
        at = (rws(h * c, h), pl.ds(p * f, f))
        pltpu.make_async_copy(wd.at[:, lanes((p * 2 + c) * f, f)], wdn.at[at], ls.at[3]).start()

    def weights_from_other():
        for y in range(2):
            for q, w in enumerate((wg, wu)):
                at = (slice(None), y, slice(None), lanes(2 * h * q + h * c, h))
                pltpu.make_async_remote_copy(
                    src_ref=w.at[y, :, 1 - c], dst_ref=wgu.at[at], send_sem=ls.at[1], recv_sem=ls.at[2],
                    device_id=other_c, device_id_type=MESH).start()
        for p in range(8):
            at = (rws(h * c, h), pl.ds(p * f, f))
            pltpu.make_async_remote_copy(
                src_ref=wd.at[:, lanes((p * 2 + 1 - c) * f, f)], dst_ref=wdn.at[at], send_sem=ls.at[4],
                recv_sem=ls.at[5], device_id=other_c, device_id_type=MESH).start()

    ready = []

    def weights_ready():
        half_gu = wgu.at[:, :, :, pl.ds(0, 2 * h)]
        half_d = wdn.at[pl.ds(0, h)]
        for i, part in ((0, half_gu), (1, half_gu), (2, half_gu), (3, half_d), (4, half_d), (5, half_d)):
            pltpu.make_async_copy(part, part, ls.at[i]).wait()

    picks = routing(cap, ids, nums, yl, z)
    for copy in taken:
        copy.wait()
    pend, local = {}, {}
    two = 2 * cap
    bufs = (tbuf, gbuf)
    sums = (pout, pback)

    def region(tokens_first, k, axes, z=zl, x=x, y=yh):
        row, n = (k * two, two) if "z" in axes else (k * two + z * cap, cap)
        if "x" in axes and "y" in axes:
            off, width = 0, d2
        elif tokens_first:
            off, width = (off_a(x, 0), 2 * f) if "y" in axes else (off_a(x, y), f)
        else:
            off, width = (off_b(y, 0), 4 * f) if "x" in axes else (off_b(y, x), f)
        return row, n, off, width

    def view(buf, part):
        row, n, off, width = part
        return buf.at[rws(row, n), lanes(off, width)]

    def halves(part):
        row, n, off, width = part
        top = -(-n // 32) * 16
        return (row, top, off, width), (row + top, n - top, off, width)

    def dispatch(k, a):
        off = (off_a(x, yh), off_b(yh, x))[a]
        theirs = 1 - zl if k % 2 else zl
        sent[a, k] = jnp.dot(picks[k][a], (tok_in, gout_in)[a][...], preferred_element_type=F32).astype(BF)
        dst = bufs[a].at[rws(k * two + theirs * cap, cap), lanes(off, f)]
        if k == 0:
            copy = pltpu.make_async_copy(sent.at[a, 0], dst, ls.at[6 + a])
            copy.start()
            local["d", a] = copy
            pend["g", k, a] = []
        else:
            pend["g", k, a] = [send(sent.at[a, k], dst, dev(**homes[k]))]
        path = GATHER[a][k]
        if path[0] == "M":
            pend["g", k, a].append(send(sent.at[a, k], dst, beside(k, path[1])))

    def gathered(k, a):
        if k == 0 and ("d", a) in local:
            local.pop(("d", a)).wait()
        got(pend["g", k, a])

    def gather(k, a, phase):
        gathered(k, a)
        axis, axes, later = gather_steps(GATHER[a][k])[phase - 1]
        buf = bufs[a]
        if axis == "x" and later:
            up = view(buf, halves(region(a == 0, k, axes, x=xl))[0])
            down = view(buf, halves(region(a == 0, k, axes, x=xr))[1])
            pend["g", k, a] = [send(up, up, right), send(down, down, left)]
        else:
            mine = view(buf, region(a == 0, k, axes))
            to = dict(x=(right, left), X=(right, left, across), y=(other_y,), z=(other_z,))[axis]
            pend["g", k, a] = [send(mine, mine, target) for target in to]

    def project_tokens(k):
        gathered(k, 0)
        rows = pl.ds(k * two, two)
        if not ready:
            weights_ready()
            ready.append(True)

        @pl.loop(0, 2)
        def _(n):
            w = wgu[:, :, :, lanes(n * 2 * h, 2 * h)].reshape(d2, 2 * h)
            act_mine[rows, lanes(n * 2 * h, 2 * h)] = jnp.dot(tbuf[rows, :], w, preferred_element_type=F32)

    def project_grads(k):
        gathered(k, 1)
        rows = pl.ds(k * two, two)
        if not ready:
            weights_ready()
            ready.append(True)

        @pl.loop(0, 2)
        def _(n):
            act_mine[rows, lanes((4 + n) * h, h)] = lax.dot_general(
                gbuf[rows, :], wdn[rws(n * h, h), :], ROWS_BOTH, preferred_element_type=F32)

    def swap(k):
        rows = pl.ds(k * two, two)
        pend["p", k] = [send(act_mine.at[rows], act_theirs.at[rows], other_c)]

    def activate(k):
        got(pend["p", k])

        @pl.loop(0, two // 16)
        def _(i):
            rows = rws(k * two + i * 16, 16)
            for n in range(2):
                def both(q):
                    at = (rows, pl.ds((q * 2 + n) * h, h))
                    return act_mine[at] + act_theirs[at]
                gate, up, grad = both(0), both(1), both(2)
                sig = jax.nn.sigmoid(gate)
                silu = gate * sig
                hid[rows, pl.ds(n * h, h)] = (silu * up).astype(BF)
                gact[rows, pl.ds(n * h, h)] = (grad * up * sig * (1.0 + gate * (1.0 - sig))).astype(BF)
                gact[rows, pl.ds((2 + n) * h, h)] = (grad * silu).astype(BF)

    def expand_out(k):
        rows = pl.ds(k * two, two)

        @pl.loop(0, 4)
        def _(n):
            at = lanes(n * 2 * f, 2 * f)
            pout[rows, at] = jnp.dot(hid[rows, :], wdn[:, at], preferred_element_type=F32).astype(BF)

    def expand_back(k):
        rows = pl.ds(k * two, two)

        @pl.loop(0, 4)
        def _(n):
            w = wgu[n].reshape(2 * f, 4 * h)
            pback[rows, lanes(n * 2 * f, 2 * f)] = lax.dot_general(
                gact[rows, :], w, ROWS_BOTH, preferred_element_type=F32).astype(BF)

    def swap_in(k, a, landed):
        got(pend["r", k, a])
        for part, slots in landed:
            row, n, off, width = part
            add_into(sums[a], row, n, off, width, *slots)

    def reduce(k, a, phase):
        if phase > 1:
            swap_in(k, a, landing[k, a])
        axis, axes, later = reduce_steps(REDUCE[a][k])[phase - 1]
        spot = functools.partial(region, a == 1, k, axes)
        slots = inbox[k, a, phase]
        if axis == "X":
            moves = [(spot(x=xr), right), (spot(x=xl), left), (spot(x=xo), across)]
            added = [(spot(), (0, 1, 2))]
        elif axis == "x" and later:
            moves, added = [(spot(x=xr), right), (spot(x=xl), left)], [(spot(), (0, 1))]
        elif axis == "x":
            moves = [(halves(spot(x=xo))[0], right), (halves(spot(x=xo))[1], left)]
            added = [(halves(spot(x=xr))[0], (0,)), (halves(spot(x=xl))[1], (1,))]
        elif axis == "y":
            moves, added = [(spot(y=1 - yh), other_y)], [(spot(), (0,))]
        else:
            moves, added = [(spot(z=1 - zl), other_z)], [(spot(), (0,))]
        pend["r", k, a] = [send(view(sums[a], part), slot, target) for (part, target), slot in zip(moves, slots)]
        landing[k, a] = [(part, [slots[j] for j in which]) for part, which in added]

    def return_home(k, a):
        swap_in(k, a, landing[k, a])
        spot = functools.partial(region, a == 1, k, "")
        mine, path = view(sums[a], spot()), REDUCE[a][k]
        pend["h", k, a] = []
        if k == 0:
            local["h", a] = pltpu.make_async_copy(mine, home.at[a, 0, 0], ls.at[8 + a])
            local["h", a].start()
        else:
            pend["h", k, a].append(send(mine, home.at[a, k, 0], dev(**homes[k])))
        if path[0] == "M":
            theirs = view(sums[a], spot(y=1 - yh) if path[1] == "y" else spot(z=1 - zl))
            pend["h", k, a].append(send(theirs, home.at[a, k, 1], beside(k, path[1])))

    def weight_grads_up(part):
        @pl.loop(part * 2, part * 2 + 2)
        def _(p):
            there = rws((((p % 2) * 4 + p // 2) * 2 + c) * f, f)
            for q, out in enumerate((gg, gu)):
                def product(core):
                    return lax.dot_general(
                        tbuf[:, lanes(p * f, f)], gact[:, lanes(2 * h * q + h * core, h)], ROWS_TOP,
                        preferred_element_type=F32).astype(BF)
                gwt[q, p] = product(1 - c)
                pltpu.make_async_remote_copy(
                    src_ref=gwt.at[q, p], dst_ref=out.at[there], send_sem=ls.at[11], recv_sem=ls.at[12],
                    device_id=other_c, device_id_type=MESH).start()
                out[there, :] = product(c)

    def weight_grads_down(part):
        @pl.loop(part * 2, part * 2 + 2)
        def _(p):
            there = lanes((p * 2 + c) * f, f)
            def product(core):
                return lax.dot_general(
                    hid[:, lanes(h * core, h)], gbuf[:, lanes(p * f, f)], ROWS_TOP,
                    preferred_element_type=F32).astype(BF)
            gdt[p] = product(1 - c)
            pltpu.make_async_remote_copy(
                src_ref=gdt.at[p], dst_ref=gd.at[:, there], send_sem=ls.at[14], recv_sem=ls.at[15],
                device_id=other_c, device_id_type=MESH).start()
            gd[:, there] = product(c)

    def weight_grads_done():
        for i, part in ((11, gwt), (12, gwt), (14, gdt), (15, gdt)):
            pltpu.make_async_copy(part, part, ls.at[i]).wait()

    steps = dict(d=dispatch, g=gather, t=project_tokens, p=project_grads, s=swap, v=activate, o=expand_out,
                 b=expand_back, r=reduce, h=return_home, w=weight_grads_up, n=weight_grads_down)
    pl.semaphore_wait(barrier, len(partners))
    drained = 0
    for i, step in enumerate(ORDER):
        steps[step[0]](*(int(digit) for digit in step[1:]))
        if i == 11:
            weights_from_other()
        old = max(len(started) - 40, 0)
        for copy in started[drained:old]:
            copy.wait_send()
        drained = old
    weight_grads_done()
    for copy in started[drained:]:
        copy.wait_send()
    for a in range(2):
        local["h", a].wait()
        for k in range(CHUNKS):
            got(pend["h", k, a])


def body(tokens, grad_out, expert_ids, gate_num, gate_weight, up_weight, down_weight):
    count, f = tokens.shape
    d, h = gate_weight.shape
    cap = 5 * count // 8
    rows, d2 = 8 * cap, 8 * f
    ids, nums = expert_ids.T, gate_num.reshape(1, count)
    split = (2, 4, 2, f, h)
    vm = pl.BlockSpec(memory_space=pltpu.VMEM)
    anywhere = pl.BlockSpec(memory_space=pl.ANY)

    def v(*shape, dtype=BF):
        return pltpu.VMEM(shape, dtype)

    def like(*shape):
        return jax.ShapeDtypeStruct(shape, BF)

    sems = 128
    home, gg, gu, gd = pl.pallas_call(
        functools.partial(kernel, cap, f, h),
        out_shape=(v(2, CHUNKS, 2, cap, f), v(d, h), v(d, h), v(h, d)),
        in_specs=[vm, vm, anywhere, anywhere, anywhere, anywhere, anywhere],
        out_specs=(vm, vm, vm, vm),
        scratch_shapes=[
            v(count, f), v(count, f), v(2, CHUNKS, cap, f), v(rows, d2), v(rows, d2),
            v(4, 2, f, 4 * h), v(2 * h, d2),
            v(rows, 6 * h, dtype=F32), v(rows, 6 * h, dtype=F32), v(rows, 2 * h), v(rows, 4 * h),
            v(rows, d2), v(rows, d2),
            v(2, 8, f, h), v(8, h, f),
            pltpu.SemaphoreType.DMA((sems,)), pltpu.SemaphoreType.DMA((sems,)), pltpu.SemaphoreType.DMA((16,)),
        ] + [v(*shape) for _, shape in boxes(cap, f)],
        compiler_params=pltpu.CompilerParams(
            collective_id=1, has_side_effects=True, vmem_limit_bytes=49 * 2**20),
        name="moe_layer",
    )(ids, nums, tokens, grad_out, gate_weight.reshape(split), up_weight.reshape(split), down_weight)

    parts = 4
    return tuple(pl.pallas_call(
        functools.partial(finish, cap, parts),
        out_shape=(like(count, f), like(count, f), like(d, h), like(d, h), like(h, d)),
        in_specs=[vm, vm, vm, vm, vm, vm],
        out_specs=(vm, vm, anywhere, anywhere, anywhere),
        scratch_shapes=[pltpu.SemaphoreType.DMA((3, parts))],
        compiler_params=pltpu.CompilerParams(vmem_limit_bytes=16 * 2**20),
        name="finish",
    )(ids, nums, home, gg, gu, gd))


def solution(mesh):
    placed = (
        P("grp", "col"),
        P("grp", "col"),
        P("grp", None),
        P("grp"),
        P(None, ("grp", "col")),
        P(None, ("grp", "col")),
        P(("grp", "col"), None),
    )
    return jax.shard_map(
        body,
        mesh=mesh,
        in_specs=placed,
        out_specs=(
            P("grp", "col"),
            P("grp", "col"),
            P(None, ("grp", "col")),
            P(None, ("grp", "col")),
            P(("grp", "col"), None),
        ),
        check_vma=False,
    )
```
